768 devices in a mesh: grid: 96 (over y, z), mem: 8 (over x, core).
Axes of the slice: x: 4, y: 8, z: 12, core: 2. Of those that a mesh axis runs over, the one named last changes fastest.
Arguments:
- background_fields: float32 [64, 12288, 128], P('mem', 'grid'), may hold values from -12 to 12
- wind_courant: float32 [12288, 128], P('grid'), may hold values from -0.4 to 0.4
- spreading_number: float32 [12288, 128], P('grid'), may hold values from 0.05 to 0.2
- obs_col: int32 [36864], P('grid'), may hold values from 0 to 127
- obs_lev: int32 [36864], P('grid'), may hold values from 0 to 127
- obs_value: float32 [36864], P('grid'), may hold values from -48 to 48
- obs_var: float32 [36864], P('grid'), may hold values from 64 to 256
Outputs:
- analysis: bfloat16 [64, 12288, 128], P('mem', 'grid')
The draws below stay inside these ranges and needn't reach their ends.
All inputs are finite; a program needn't handle non-finite values.
Results may differ from the reference program's by a relative error of at most 0.0055.
Values may be sent and summed in bfloat16 or wider, within the bound.
No kernel may reach another device: no remote copies, remote signals or barrier semaphores. Data moves between devices by JAX's collectives and lax.ppermute only.
A program may use at most 32 MiB of HBM per device.

```python
import math
import jax
import jax.numpy as jnp
from jax import lax

PARTICIPANTS = 64
HEIGHT_LAYERS = 128
CX = 128
OBS_DEV = 384
NSITER = 8
GRID_PILLARS = 12288
NOBS = 36864


def draw_background_fields(key, part):
    key = jax.random.fold_in(key, 7)
    keys = jax.random.split(key, 4)
    place = (jnp.arange(GRID_PILLARS, dtype=jnp.float32) + 0.5) / GRID_PILLARS
    base = jax.random.normal(keys[0], (PARTICIPANTS, GRID_PILLARS, HEIGHT_LAYERS), jnp.float32)
    spread = jnp.exp(jax.random.uniform(keys[1], (PARTICIPANTS,), jnp.float32, math.log(0.4), math.log(2.5)))
    slope = jnp.sqrt(0.5 + place)
    centre_box = jax.random.normal(keys[2], (GRID_PILLARS, HEIGHT_LAYERS), jnp.float32)
    partner = jax.random.permutation(keys[3], PARTICIPANTS)
    paired = (base + 0.8 * base[partner]) / math.sqrt(1.64)
    field = centre_box[None, :, :] + spread[:, None, None] * slope[None, :, None] * paired
    return jnp.clip(field, -12.0, 12.0)


def touch_ends(result, key, smallest, largest):
    longest = result.shape.index(max(result.shape))
    spots = []
    for shift in (0, 1):
        where = [jax.random.randint(jax.random.fold_in(key, axis), (), 0, length) for axis, length in enumerate(result.shape)]
        where[longest] = (where[longest] + shift) % result.shape[longest]
        spots.append(tuple(where))
    return result.at[spots[0]].set(smallest).at[spots[1]].set(largest)


def shard_levels(rng, extent, cuts, least, high):
    factor_of = 1.0
    for axis_at, blocks in cuts:
        steps = jax.random.uniform(jax.random.fold_in(jax.random.fold_in(rng, 6), axis_at), (blocks,), jnp.float32, least / len(cuts), high / len(cuts))
        factor_of = factor_of * jnp.repeat(jnp.exp(steps), extent[axis_at] // blocks).reshape((-1,) + (1,) * (len(extent) - 1 - axis_at))
    return factor_of


def gaussian(rng, dims, scale, reach, cuts=(), kind=jnp.bfloat16):
    result = jax.random.normal(rng, dims, jnp.float32) * scale
    if len(cuts) > 0:
        result = shard_levels(rng, dims, cuts, -0.22, 0.18) * result
    return jnp.clip(result, min=-reach, max=reach).astype(kind)


def setup_inputs(seed: int = 0) -> dict:
    streams_of = jax.random.split(jax.random.key(seed), 8)
    return {
        "background_fields": draw_background_fields(jax.random.fold_in(streams_of[7], 71), 0),
        "wind_courant": jnp.clip(jax.random.uniform(streams_of[1], (GRID_PILLARS, HEIGHT_LAYERS), jnp.float32, -0.4, 0.4) * shard_levels(streams_of[1], (GRID_PILLARS, HEIGHT_LAYERS), ((0, 96),), -0.4, 0.0), -0.4, 0.4),
        "spreading_number": jnp.clip(0.05 + 0.15 * jax.random.uniform(streams_of[2], (GRID_PILLARS, HEIGHT_LAYERS), jnp.float32) ** shard_levels(streams_of[2], (GRID_PILLARS, HEIGHT_LAYERS), ((0, 96),), -0.2, 0.2), 0.05, 0.2),
        "obs_col": touch_ends(jax.random.randint(streams_of[3], (NOBS,), 0, CX), jax.random.fold_in(streams_of[3], 1), 0, CX - 1).astype(jnp.int32),
        "obs_lev": touch_ends(jax.random.randint(streams_of[4], (NOBS,), 0, HEIGHT_LAYERS), jax.random.fold_in(streams_of[4], 1), 0, HEIGHT_LAYERS - 1).astype(jnp.int32),
        "obs_value": gaussian(streams_of[5], (NOBS,), 8.0, 48.0, ((0, 96),), jnp.float32),
        "obs_var": jnp.clip(jnp.exp(math.log(256.0) - 1.3862944 * jax.random.uniform(streams_of[6], (NOBS,), jnp.float32) ** shard_levels(streams_of[6], (NOBS,), ((0, 96),), -0.2, 0.2)), 64.0, 256.0),
    }


def inverse_root(amat, count, iters):
    scale = jnp.sqrt(jnp.sum(amat * amat))
    eye = jnp.eye(count, dtype=jnp.float32)
    yit = amat / scale
    zit = eye
    for step in range(iters):
        tmat = (3.0 * eye - jnp.dot(zit, yit, precision=lax.Precision.HIGHEST)) / 2.0
        yit = jnp.dot(yit, tmat, precision=lax.Precision.HIGHEST)
        zit = jnp.dot(tmat, zit, precision=lax.Precision.HIGHEST)
    return zit / jnp.sqrt(scale)

def build_mix(gram, proj, count, iters):
    amat = (count - 1.0) * jnp.eye(count, dtype=jnp.float32) + gram
    root = inverse_root(amat, count, iters)
    inner = jnp.dot(root, proj, precision=lax.Precision.HIGHEST)
    wmean = jnp.dot(root, inner, precision=lax.Precision.HIGHEST)
    tfm = wmean[:, None] + jnp.sqrt(count - 1.0) * root
    blend_factors = 1.0 / count + tfm - lax.optimization_barrier(jnp.mean(tfm, axis=0, keepdims=True))
    return blend_factors.astype(jnp.bfloat16)

def reference(background_fields, wind_courant, spreading_number, obs_col, obs_lev, obs_value, obs_var):
    padded = jnp.pad(background_fields, ((0, 0), (1, 1), (1, 1)))
    centre_box = padded[:, 1:-1, 1:-1]
    left_box = padded[:, :-2, 1:-1]
    right_box = padded[:, 2:, 1:-1]
    below_layer = padded[:, 1:-1, :-2]
    above_layer = padded[:, 1:-1, 2:]
    advance_model = centre_box + wind_courant * (left_box - right_box) / 2.0 + spreading_number * (right_box + left_box + above_layer + below_layer - 4.0 * centre_box)
    block = (jnp.arange(NOBS, dtype=jnp.int32) // OBS_DEV).astype(jnp.int32)
    flattened_position = ((block * CX + obs_col) * HEIGHT_LAYERS + obs_lev).astype(jnp.int32)
    expected_readings = jnp.take(advance_model.reshape(PARTICIPANTS, GRID_PILLARS * HEIGHT_LAYERS), flattened_position, axis=1)
    ybar = lax.optimization_barrier(jnp.mean(expected_readings, axis=0))
    anomaly = expected_readings - ybar
    innov = obs_value - ybar
    weighted = anomaly / obs_var
    gram = jnp.dot(weighted, anomaly.T, precision=lax.Precision.HIGHEST)
    proj = jnp.dot(weighted, innov, precision=lax.Precision.HIGHEST)
    blend_factors = build_mix(gram, proj, PARTICIPANTS, NSITER)
    participant_fields = advance_model.astype(jnp.bfloat16).reshape(PARTICIPANTS, GRID_PILLARS * HEIGHT_LAYERS)
    analysis = jnp.dot(blend_factors.T, participant_fields, preferred_element_type=jnp.float32)
    return analysis.astype(jnp.bfloat16).reshape(PARTICIPANTS, GRID_PILLARS, HEIGHT_LAYERS)
```

```python
import jax
import jax.numpy as jnp
from jax import lax
from jax.sharding import Mesh, PartitionSpec as P

NSITER = 8
ROWS = 8


def extended(block, sides, width):
    for axis, dim in sides:
        count = lax.axis_size(axis)
        forward = [(i, i + 1) for i in range(count - 1)]
        backward = [(target, source) for source, target in forward]
        low = lax.ppermute(
            lax.slice_in_dim(block, block.shape[dim] - width, None, axis=dim), axis, forward
        )
        high = lax.ppermute(lax.slice_in_dim(block, 0, width, axis=dim), axis, backward)
        block = jnp.concatenate([low, block, high], axis=dim)
    return block


def inverse_root(amat, count, iters):
    scale = jnp.sqrt(jnp.sum(amat * amat))
    eye = jnp.eye(count, dtype=jnp.float32)
    yit = amat / scale
    zit = eye
    for step in range(iters):
        tmat = (3.0 * eye - jnp.dot(zit, yit, precision=lax.Precision.HIGHEST)) / 2.0
        yit = jnp.dot(yit, tmat, precision=lax.Precision.HIGHEST)
        zit = jnp.dot(tmat, zit, precision=lax.Precision.HIGHEST)
    return zit / jnp.sqrt(scale)


def build_mix(gram, proj, count, iters):
    amat = (count - 1.0) * jnp.eye(count, dtype=jnp.float32) + gram
    root = inverse_root(amat, count, iters)
    inner = jnp.dot(root, proj, precision=lax.Precision.HIGHEST)
    wmean = jnp.dot(root, inner, precision=lax.Precision.HIGHEST)
    tfm = wmean[:, None] + jnp.sqrt(count - 1.0) * root
    blend_factors = 1.0 / count + tfm - jnp.mean(tfm, axis=0, keepdims=True)
    return blend_factors.astype(jnp.bfloat16)


def adjacent_increment(field, padded_border, wind_courant, spreading_number):
    left_box = padded_border[:, :-2, :]
    right_box = padded_border[:, 2:, :]
    vertical = jnp.pad(field, ((0, 0), (0, 0), (1, 1)))
    below_layer = vertical[:, :, :-2]
    above_layer = vertical[:, :, 2:]
    return (
        field
        + wind_courant * (left_box - right_box) / 2.0
        + spreading_number * (right_box + left_box + above_layer + below_layer - 4.0 * field)
    )


def exchange_sum(part, axis):
    copies = jnp.broadcast_to(part[None], (lax.axis_size(axis),) + part.shape)
    return jnp.sum(lax.all_to_all(copies, axis, 0, 0), axis=0)


def summed(gram_part, proj_part, axis):
    half = gram_part.shape[0] // 2
    packed = jnp.concatenate(
        [
            jnp.concatenate([gram_part[:half], gram_part[half:]], axis=1),
            jnp.pad(proj_part[None], ((0, 7), (0, half * 2))),
        ],
        axis=0,
    )
    for part in ("row", "col"):
        packed = exchange_sum(packed, part)
    gram = jnp.concatenate([packed[:half, : 2 * half], packed[:half, 2 * half :]], axis=0)
    return gram, packed[half, : 2 * half]


def member_path(
    background_fields, wind_courant, spreading_number, obs_col, obs_lev, obs_value, obs_var
):
    participant_piece, pillar_amount, layer_amount = background_fields.shape
    members = participant_piece * lax.axis_size("mem")
    padded_border = extended(background_fields, ((("row", "col"), 1),), 1)
    advance_model = adjacent_increment(
        background_fields, padded_border, wind_courant, spreading_number
    )
    flattened_position = obs_col * layer_amount + obs_lev
    local_predicted_observations = jnp.take(
        advance_model.reshape(participant_piece, pillar_amount * layer_amount),
        flattened_position,
        axis=1,
    )
    count = lax.axis_size("mem")
    copies = jnp.broadcast_to(
        local_predicted_observations[None], (count,) + local_predicted_observations.shape
    )
    expected_readings = lax.all_to_all(copies, "mem", 0, 0).reshape(members, -1)
    ybar = jnp.mean(expected_readings, axis=0)
    anomaly = expected_readings - ybar
    innov = obs_value - ybar
    weighted = anomaly / obs_var
    gram_part = jnp.dot(weighted, anomaly.T, precision=lax.Precision.HIGHEST)
    proj_part = jnp.dot(weighted, innov, precision=lax.Precision.HIGHEST)
    gram, proj = summed(gram_part, proj_part, "grid")
    blend_factors = build_mix(gram, proj, members, NSITER)
    return (advance_model.astype(jnp.bfloat16), blend_factors)


def on_device(
    background_fields, wind_courant, spreading_number, obs_col, obs_lev, obs_value, obs_var
):
    participant_piece, pillar_amount, layer_amount = background_fields.shape
    participant_fields, blend_factors = member_path(
        background_fields, wind_courant, spreading_number, obs_col, obs_lev, obs_value, obs_var
    )
    first_own = lax.axis_index("mem") * participant_piece
    piece = lax.all_gather(participant_fields, "mem", axis=0, tiled=True)
    rows = piece.shape[0]
    block = lax.dynamic_slice(blend_factors, (0, first_own), (rows, participant_piece))
    flat_piece = piece.reshape(rows, pillar_amount * layer_amount)
    total = jnp.dot(block.T, flat_piece, preferred_element_type=jnp.float32)
    analysis = total.astype(jnp.bfloat16).reshape(participant_piece, pillar_amount, layer_amount)
    return analysis


def solution(mesh):
    grid, mem = mesh.shape["grid"], mesh.shape["mem"]
    fine = Mesh(mesh.devices.reshape(ROWS, grid // ROWS, mem), ("row", "col", "mem"))
    blocks = ("row", "col")
    in_specs = (
        P("mem", blocks, None),
        P(blocks, None),
        P(blocks, None),
        P(blocks),
        P(blocks),
        P(blocks),
        P(blocks),
    )
    out_specs = P("mem", blocks, None)
    return jax.shard_map(
        on_device, mesh=fine, in_specs=in_specs, out_specs=out_specs, check_vma=False
    )
```

```python
import functools

import jax
import jax.numpy as jnp
from jax import lax
from jax.experimental import pallas as pl
from jax.experimental.pallas import tpu as pltpu
from jax.sharding import Mesh, PartitionSpec as P

NSITER = 8
ROWS = 8
LANES = 128
GROUP = 8
EXACT = lax.Precision.HIGHEST
VMEM = pl.BlockSpec(memory_space=pltpu.VMEM)


def lane_index(rows):
    return lax.broadcasted_iota(jnp.int32, (rows, LANES), 1)


def neighbours(block, axis):
    count = lax.axis_size(axis)
    forward = [(i, i + 1) for i in range(count - 1)]
    backward = [(target, source) for source, target in forward]
    last = block.shape[1] - 1
    low = lax.ppermute(block[:, last:, :], axis, forward)
    high = lax.ppermute(block[:, :1, :], axis, backward)
    return low[:, 0], high[:, 0]


def forecast_kernel(columns, field, low, high, courant, spreading, col, lev, fields, readings, cells):
    members, layers = low.shape
    lane = lax.broadcasted_iota(jnp.int32, (members, layers), 1)

    def column(i):
        return field[pl.ds(i, members, stride=columns), :]

    def advance(i, left, centre, right):
        below = jnp.where(lane == 0, 0.0, pltpu.roll(centre, 1, 1))
        above = jnp.where(lane == layers - 1, 0.0, pltpu.roll(centre, layers - 1, 1))
        wind = courant[pl.ds(i, 1), :]
        spread = spreading[pl.ds(i, 1), :]
        value = (
            centre
            + wind * (left - right) * 0.5
            + spread * (right + left + above + below - 4.0 * centre)
        )
        cells[i * members : (i + 1) * members, :] = value
        fields[:, i * layers : (i + 1) * layers] = value.astype(jnp.bfloat16)

    left, centre = low[...], column(0)
    for i in range(columns):
        right = column(i + 1) if i + 1 < columns else high[...]
        advance(i, left, centre, right)
        left, centre = centre, right

    observations = col.shape[1]
    level = lax.broadcasted_iota(jnp.int32, (layers, observations), 0)
    chosen = jnp.where(level == lev[...], 1.0, 0.0).astype(jnp.bfloat16)
    where_col = jnp.broadcast_to(col[...], (members, observations))
    step = 16
    total = jnp.zeros((members, observations), jnp.float32)
    for base in range(0, columns, step):
        rest = cells[base * members : (base + step) * members, :]
        picked = None
        for _ in range(3):
            part = rest.astype(jnp.bfloat16)
            rest = rest - part.astype(jnp.float32)
            term = jnp.dot(part, chosen, preferred_element_type=jnp.float32)
            picked = term if picked is None else picked + term
        for i in range(step):
            row = picked[i * members : (i + 1) * members, :]
            total = total + jnp.where(where_col == base + i, row, 0.0)
    readings[...] = total


def forecast(field, low, high, courant, spreading, col, lev):
    members, columns, layers = field.shape
    observations = col.shape[0]
    return pl.pallas_call(
        functools.partial(forecast_kernel, columns),
        out_shape=(
            jax.ShapeDtypeStruct((members, columns * layers), jnp.bfloat16),
            jax.ShapeDtypeStruct((members, observations), jnp.float32),
        ),
        in_specs=[VMEM] * 7,
        out_specs=(VMEM, VMEM),
        scratch_shapes=[pltpu.VMEM((members * columns, layers), jnp.float32)],
        compiler_params=pltpu.CompilerParams(vmem_limit_bytes=16 * 2**20),
        name="forecast",
    )(
        field.reshape(members * columns, layers),
        low,
        high,
        courant,
        spreading,
        col.reshape(1, observations),
        lev.reshape(1, observations),
    )


def pack(upper, proj_row):
    lane = lane_index(GROUP)
    row = [upper[GROUP * r : GROUP * (r + 1), :] for r in range(8)]
    roll = lambda r, shift: pltpu.roll(row[r], shift, 1)
    first = jnp.where(lane < 64, row[0], roll(1, 64))
    second = jnp.where(lane < 16, roll(7, 80), row[2])
    second = jnp.where(lane >= 64, roll(3, 48), second)
    second = jnp.where(lane >= 112, roll(6, 64), second)
    third = jnp.where(lane < 32, roll(5, 96), row[4])
    third = jnp.where(lane >= 64, pltpu.roll(proj_row, 64, 1), third)
    return first, second, third


def unpack(first, second, third):
    lane = lane_index(GROUP)
    roll = lambda part, shift: pltpu.roll(part, shift, 1)
    rows = [
        first,
        roll(first, 64),
        second,
        roll(second, 80),
        third,
        roll(third, 32),
        roll(second, 64),
        roll(second, 48),
    ]
    keep = [
        jnp.where((lane >= 16 * (r // 2)) & (lane < 64), part, 0.0) for r, part in enumerate(rows)
    ]
    upper = jnp.concatenate(keep, axis=0)
    return upper, roll(third, 64)[:1, :]


def gram_kernel(members, readings, value, var, copies):
    hx = readings[...]
    ybar = jnp.sum(hx, axis=0, keepdims=True) * (1.0 / members)
    anomaly = hx - ybar
    innov = value[...] - ybar
    weighted = anomaly / var[...]
    pad = jnp.zeros((LANES - members, hx.shape[1]), jnp.float32)
    weighted = jnp.concatenate([weighted, pad], axis=0)
    nt = (((1,), (1,)), ((), ()))
    gram = lax.dot_general(
        anomaly, weighted, nt, precision=EXACT, preferred_element_type=jnp.float32
    )
    rows = jnp.where(
        lax.broadcasted_iota(jnp.int32, (GROUP, hx.shape[1]), 0) == 0,
        jnp.broadcast_to(innov, (GROUP, hx.shape[1])),
        0.0,
    )
    proj = lax.dot_general(
        rows, weighted, nt, precision=EXACT, preferred_element_type=jnp.float32
    )
    for s, part in enumerate(pack(gram, proj)):
        for r in range(copies.shape[0]):
            copies[r, GROUP * s : GROUP * (s + 1), :] = part


def gram_parts(readings, value, var, count):
    members, observations = readings.shape
    return pl.pallas_call(
        functools.partial(gram_kernel, members),
        out_shape=jax.ShapeDtypeStruct((count, 3 * GROUP, LANES), jnp.float32),
        in_specs=[VMEM] * 3,
        out_specs=VMEM,
        name="gram",
    )(readings, value.reshape(1, observations), var.reshape(1, observations))


def sum_kernel(parts, copies):
    total = parts[0]
    for r in range(1, parts.shape[0]):
        total = total + parts[r]
    for r in range(copies.shape[0]):
        copies[r] = total


def sum_copies(parts, count):
    return pl.pallas_call(
        sum_kernel,
        out_shape=jax.ShapeDtypeStruct((count,) + parts.shape[1:], jnp.float32),
        in_specs=[VMEM],
        out_specs=VMEM,
        name="row_sum",
    )(parts)


def analysis_kernel(members, iters, own, parts, fields, out, held, mixed, cells, sem):
    fetch = pltpu.make_async_copy(fields, held, sem)
    fetch.start()

    total = parts[0]
    for r in range(1, parts.shape[0]):
        total = total + parts[r]
    upper, proj = unpack(*[total[GROUP * s : GROUP * (s + 1), :] for s in range(3)])
    square = jnp.concatenate(
        [upper, jnp.zeros((LANES - members, LANES), jnp.float32)], axis=0
    )
    turned = square.T
    row = lax.broadcasted_iota(jnp.int32, (LANES, LANES), 0)
    lane = lane_index(LANES)
    gram = jnp.where(lane // 16 >= row // 16, square, turned)[:members, :members]
    row, lane = row[:members, :members], lane[:members, :members]
    eye = jnp.where(row == lane, 1.0, 0.0)
    proj = proj[:, :members]

    dot = lambda a, b: jnp.dot(a, b, precision=EXACT, preferred_element_type=jnp.float32)
    amat = (members - 1.0) * eye + gram
    scale = jnp.sqrt(jnp.sum(amat * amat, keepdims=True))
    yit = amat / scale
    zit = eye
    for step in range(iters):
        if step == 0:
            tmat = (3.0 * eye - yit) * 0.5
        else:
            tmat = (3.0 * eye - dot(zit, yit)) * 0.5
        if step + 1 < iters:
            yit = dot(yit, tmat)
        zit = tmat if step == 0 else dot(tmat, zit)
    root = zit / jnp.sqrt(scale)
    turned = root.T
    wmean = dot(dot(proj, turned), turned)
    tfm = wmean + jnp.sqrt(jnp.float32(members - 1.0)) * turned
    centre = jnp.sum(tfm, axis=1, keepdims=True) * (1.0 / members)
    mixed[...] = 1.0 / members + tfm - centre

    count, columns, layers = out.shape
    mine = mixed[pl.ds(pl.multiple_of(own[0] * count, count), count), :].astype(jnp.bfloat16)
    fetch.wait()
    step = 16
    for base in range(0, columns, step):
        block = jnp.dot(
            mine,
            held[:, base * layers : (base + step) * layers],
            preferred_element_type=jnp.float32,
        )
        for i in range(step):
            cells[pl.ds(base + i, count, stride=columns), :] = block[
                :, i * layers : (i + 1) * layers
            ]
    out[...] = cells[...].astype(jnp.bfloat16).reshape(out.shape)


def analysis(own, parts, fields, shape):
    members = fields.shape[0]
    count, columns, layers = shape
    return pl.pallas_call(
        functools.partial(analysis_kernel, members, NSITER),
        out_shape=jax.ShapeDtypeStruct(shape, jnp.bfloat16),
        in_specs=[
            pl.BlockSpec(memory_space=pltpu.SMEM),
            VMEM,
            pl.BlockSpec(memory_space=pl.ANY),
        ],
        out_specs=VMEM,
        scratch_shapes=[
            pltpu.VMEM(fields.shape, jnp.bfloat16),
            pltpu.VMEM((members, members), jnp.float32),
            pltpu.VMEM((count * columns, layers), jnp.float32),
            pltpu.SemaphoreType.DMA,
        ],
        compiler_params=pltpu.CompilerParams(vmem_limit_bytes=60 * 2**20),
        name="analysis",
    )(own, parts, fields)


def on_device(
    background_fields, wind_courant, spreading_number, obs_col, obs_lev, obs_value, obs_var
):
    own = background_fields.shape[0]
    low, high = neighbours(background_fields, ("row", "col"))
    fields, hx = forecast(
        background_fields, low, high, wind_courant, spreading_number, obs_col, obs_lev
    )
    everyone = lax.all_gather(fields, "mem", axis=0, tiled=True)
    mems, cols, rows = (lax.axis_size(a) for a in ("mem", "col", "row"))
    copies = jnp.broadcast_to(hx[None], (mems,) + hx.shape)
    readings = lax.all_to_all(copies, "mem", 0, 0).reshape(mems * own, hx.shape[1])
    parts = gram_parts(readings, obs_value, obs_var, rows)
    parts = lax.all_to_all(parts, "row", 0, 0)
    parts = sum_copies(parts, cols)
    parts = lax.all_to_all(parts, "col", 0, 0)
    index = lax.axis_index("mem").astype(jnp.int32).reshape(1)
    return analysis(index, parts, everyone, background_fields.shape)


def solution(mesh):
    grid, mem = mesh.shape["grid"], mesh.shape["mem"]
    fine = Mesh(mesh.devices.reshape(ROWS, grid // ROWS, mem), ("row", "col", "mem"))
    blocks = ("row", "col")
    in_specs = (
        P("mem", blocks, None),
        P(blocks, None),
        P(blocks, None),
        P(blocks),
        P(blocks),
        P(blocks),
        P(blocks),
    )
    out_specs = P("mem", blocks, None)
    return jax.shard_map(
        on_device, mesh=fine, in_specs=in_specs, out_specs=out_specs, check_vma=False
    )
```

```python
import functools

import jax
import jax.numpy as jnp
from jax import lax
from jax.experimental import pallas as pl
from jax.experimental.pallas import tpu as pltpu
from jax.sharding import Mesh, PartitionSpec as P

NSITER = 8
ROWS = 8
LANES = 128
GROUP = 8
ORDER = (0, 2, 6, 4, 1, 3, 7, 5)
EXACT = lax.Precision.HIGHEST
VMEM = pl.BlockSpec(memory_space=pltpu.VMEM)
SMALL = pltpu.CompilerParams(vmem_limit_bytes=16 * 2**20)


def lane_index(rows):
    return lax.broadcasted_iota(jnp.int32, (rows, LANES), 1)


def neighbours(block, axis):
    count = lax.axis_size(axis)
    forward = [(i, i + 1) for i in range(count - 1)]
    backward = [(target, source) for source, target in forward]
    last = block.shape[1] - 1
    low = lax.ppermute(block[:, last:, :], axis, forward)
    high = lax.ppermute(block[:, :1, :], axis, backward)
    return low[:, 0], high[:, 0]


def chosen_levels(lev, layers):
    level = lax.broadcasted_iota(jnp.int32, (layers, lev.shape[0]), 0)
    return jnp.where(level == lev[...].reshape(1, -1), 1.0, 0.0).astype(jnp.bfloat16)


def at_levels(values, chosen):
    rest, picked = values, None
    for _ in range(3):
        part = rest.astype(jnp.bfloat16)
        rest = rest - part.astype(jnp.float32)
        term = jnp.dot(part, chosen, preferred_element_type=jnp.float32)
        picked = term if picked is None else picked + term
    return picked


def inner_kernel(
    columns, field_hbm, courant_hbm, spreading_hbm, col, lev, fields, readings, edges,
    field, courant, spreading, cells, sems,
):
    sources = ((field_hbm, field), (courant_hbm, courant), (spreading_hbm, spreading))
    fetches = [pltpu.make_async_copy(s, d, sems.at[i]) for i, (s, d) in enumerate(sources)]
    for fetch in fetches:
        fetch.start()
    members = fields.shape[0]
    layers = field.shape[1]
    observations = col.shape[0]
    lane = lax.broadcasted_iota(jnp.int32, (members, layers), 1)
    chosen = chosen_levels(lev, layers)
    where_col = jnp.broadcast_to(col[...].reshape(1, -1), (members, observations))
    for fetch in fetches:
        fetch.wait()

    def column(i):
        if i < 0 or i >= columns:
            return jnp.zeros((members, layers), jnp.float32)
        return field[pl.ds(i, members, stride=columns), :]

    left, centre = column(-1), column(0)
    for i in range(columns):
        right = column(i + 1)
        below = jnp.where(lane == 0, 0.0, pltpu.roll(centre, 1, 1))
        above = jnp.where(lane == layers - 1, 0.0, pltpu.roll(centre, layers - 1, 1))
        value = (
            centre
            + courant[pl.ds(i, 1), :] * (left - right) * 0.5
            + spreading[pl.ds(i, 1), :] * (right + left + above + below - 4.0 * centre)
        )
        cells[i * members : (i + 1) * members, :] = value
        fields[:, i * layers : (i + 1) * layers] = value.astype(jnp.bfloat16)
        left, centre = centre, right

    last = columns - 1
    spread = lambda row: jnp.broadcast_to(row, (members, layers))
    edges[0] = cells[:members, :]
    edges[1] = cells[last * members :, :]
    edges[2] = spread(spreading[:1, :] + courant[:1, :] * 0.5)
    edges[3] = spread(spreading[last:, :] - courant[last:, :] * 0.5)

    step = 16
    total = jnp.zeros((members, observations), jnp.float32)
    for base in range(0, columns, step):
        picked = at_levels(cells[base * members : (base + step) * members, :], chosen)
        for i in range(step):
            if 0 < base + i < last:
                row = picked[i * members : (i + 1) * members, :]
                total = total + jnp.where(where_col == base + i, row, 0.0)
    readings[...] = total


def inner_forecast(field, courant, spreading, col, lev):
    members, columns, layers = field.shape
    observations = col.shape[0]
    anywhere = pl.BlockSpec(memory_space=pltpu.HBM)
    return pl.pallas_call(
        functools.partial(inner_kernel, columns),
        out_shape=(
            jax.ShapeDtypeStruct((members, columns * layers), jnp.bfloat16),
            jax.ShapeDtypeStruct((members, observations), jnp.float32),
            jax.ShapeDtypeStruct((4, members, layers), jnp.float32),
        ),
        in_specs=[anywhere] * 3 + [VMEM] * 2,
        out_specs=(VMEM, VMEM, VMEM),
        scratch_shapes=[
            pltpu.VMEM((members * columns, layers), jnp.float32),
            pltpu.VMEM((columns, layers), jnp.float32),
            pltpu.VMEM((columns, layers), jnp.float32),
            pltpu.VMEM((members * columns, layers), jnp.float32),
            pltpu.SemaphoreType.DMA((3,)),
        ],
        compiler_params=SMALL,
        cost_estimate=pl.CostEstimate(
            flops=6 * members * columns * layers * observations,
            bytes_accessed=4 * members * columns * layers,
            transcendentals=0,
        ),
        name="inner_forecast",
    )(field.reshape(members * columns, layers), courant, spreading, col, lev)


def edge_kernel(columns, edges, low, high, readings, col, lev, fields_in, fields, copies):
    del fields_in
    members, layers = low.shape
    observations = col.shape[0]
    first = edges[0] + edges[2] * low[...]
    last = edges[1] + edges[3] * high[...]
    fields[:, :layers] = first.astype(jnp.bfloat16)
    fields[:, (columns - 1) * layers :] = last.astype(jnp.bfloat16)
    picked = at_levels(jnp.concatenate([first, last], axis=0), chosen_levels(lev, layers))
    where_col = jnp.broadcast_to(col[...].reshape(1, -1), (members, observations))
    total = jnp.where(where_col == 0, picked[:members, :], readings[...])
    total = jnp.where(where_col == columns - 1, picked[members:, :], total)
    for r in range(copies.shape[0]):
        copies[r] = total


def edge_forecast(columns, edges, low, high, readings, col, lev, fields, count):
    return pl.pallas_call(
        functools.partial(edge_kernel, columns),
        out_shape=(
            jax.ShapeDtypeStruct(fields.shape, fields.dtype),
            jax.ShapeDtypeStruct((count,) + readings.shape, jnp.float32),
        ),
        in_specs=[VMEM] * 7,
        out_specs=(VMEM, VMEM),
        input_output_aliases={6: 0},
        compiler_params=SMALL,
        name="edge_forecast",
    )(edges, low, high, readings, col, lev, fields)


def pack(upper, proj_row):
    lane = lane_index(GROUP)
    row = [upper[GROUP * r : GROUP * (r + 1), :] for r in range(8)]
    roll = lambda r, shift: pltpu.roll(row[r], shift, 1)
    first = jnp.where(lane < 64, row[0], roll(1, 64))
    second = jnp.where(lane < 16, roll(7, 80), row[2])
    second = jnp.where(lane >= 64, roll(3, 48), second)
    second = jnp.where(lane >= 112, roll(6, 64), second)
    third = jnp.where(lane < 32, roll(5, 96), row[4])
    third = jnp.where(lane >= 64, pltpu.roll(proj_row, 64, 1), third)
    return first, second, third


def unpack(first, second, third):
    lane = lane_index(GROUP)
    roll = lambda part, shift: pltpu.roll(part, shift, 1)
    rows = [
        first,
        roll(first, 64),
        second,
        roll(second, 80),
        third,
        roll(third, 32),
        roll(second, 64),
        roll(second, 48),
    ]
    keep = [
        jnp.where((lane >= 16 * (r // 2)) & (lane < 64), part, 0.0) for r, part in enumerate(rows)
    ]
    upper = jnp.concatenate(keep, axis=0)
    return upper, roll(third, 64)[:1, :]


def gram_kernel(me, readings, value, var, copies):
    hx = jnp.concatenate([readings[me[0] ^ code] for code in ORDER], axis=0)
    members = hx.shape[0]
    ybar = jnp.sum(hx, axis=0, keepdims=True) * (1.0 / members)
    anomaly = hx - ybar
    innov = value[...].reshape(1, -1) - ybar
    weighted = anomaly / var[...].reshape(1, -1)
    pad = jnp.zeros((LANES - members, hx.shape[1]), jnp.float32)
    weighted = jnp.concatenate([weighted, pad], axis=0)
    nt = (((1,), (1,)), ((), ()))
    gram = lax.dot_general(
        anomaly, weighted, nt, precision=EXACT, preferred_element_type=jnp.float32
    )
    rows = jnp.where(
        lax.broadcasted_iota(jnp.int32, (GROUP, hx.shape[1]), 0) == 0,
        jnp.broadcast_to(innov, (GROUP, hx.shape[1])),
        0.0,
    )
    proj = lax.dot_general(
        rows, weighted, nt, precision=EXACT, preferred_element_type=jnp.float32
    )
    for s, part in enumerate(pack(gram, proj)):
        for r in range(copies.shape[0]):
            copies[r, GROUP * s : GROUP * (s + 1), :] = part


def gram_parts(me, readings, value, var, count):
    return pl.pallas_call(
        gram_kernel,
        out_shape=jax.ShapeDtypeStruct((count, 3 * GROUP, LANES), jnp.float32),
        in_specs=[pl.BlockSpec(memory_space=pltpu.SMEM)] + [VMEM] * 3,
        out_specs=VMEM,
        compiler_params=SMALL,
        name="gram",
    )(me, readings, value, var)


def sum_kernel(parts, copies):
    total = parts[0]
    for r in range(1, parts.shape[0]):
        total = total + parts[r]
    for r in range(copies.shape[0]):
        copies[r] = total


def sum_copies(parts, count):
    return pl.pallas_call(
        sum_kernel,
        out_shape=jax.ShapeDtypeStruct((count,) + parts.shape[1:], jnp.float32),
        in_specs=[VMEM],
        out_specs=VMEM,
        compiler_params=SMALL,
        name="row_sum",
    )(parts)


def analysis_kernel(members, iters, parts, *refs):
    *fields, out, cells = refs
    total = parts[0]
    for r in range(1, parts.shape[0]):
        total = total + parts[r]
    upper, proj = unpack(*[total[GROUP * s : GROUP * (s + 1), :] for s in range(3)])
    square = jnp.concatenate(
        [upper, jnp.zeros((LANES - members, LANES), jnp.float32)], axis=0
    )
    turned = square.T
    row = lax.broadcasted_iota(jnp.int32, (LANES, LANES), 0)
    lane = lane_index(LANES)
    gram = jnp.where(lane // 16 >= row // 16, square, turned)[:members, :members]
    row, lane = row[:members, :members], lane[:members, :members]
    eye = jnp.where(row == lane, 1.0, 0.0)
    proj = proj[:, :members]

    dot = lambda a, b: jnp.dot(a, b, precision=EXACT, preferred_element_type=jnp.float32)
    amat = (members - 1.0) * eye + gram
    scale = jnp.sqrt(jnp.sum(amat * amat, keepdims=True))
    yit = amat / scale
    zit = eye
    for step in range(iters):
        if step == 0:
            tmat = (3.0 * eye - yit) * 0.5
        else:
            tmat = (3.0 * eye - dot(zit, yit)) * 0.5
        if step + 1 < iters:
            yit = dot(yit, tmat)
        zit = tmat if step == 0 else dot(tmat, zit)
    root = zit / jnp.sqrt(scale)
    turned = root.T
    wmean = dot(dot(proj, turned), turned)
    tfm = wmean + jnp.sqrt(jnp.float32(members - 1.0)) * turned
    centre = jnp.sum(tfm, axis=1, keepdims=True) * (1.0 / members)
    mixed = 1.0 / members + tfm - centre

    count, columns, layers = out.shape
    mine = mixed[:count, :].astype(jnp.bfloat16)
    step = 16
    for base in range(0, columns, step):
        held = [part[:, base * layers : (base + step) * layers] for part in fields]
        block = jnp.dot(
            mine, jnp.concatenate(held, axis=0), preferred_element_type=jnp.float32
        )
        for i in range(step):
            cells[pl.ds(base + i, count, stride=columns), :] = block[
                :, i * layers : (i + 1) * layers
            ]
    out[...] = cells[...].astype(jnp.bfloat16).reshape(out.shape)


def analysis(parts, fields, shape):
    members = sum(part.shape[0] for part in fields)
    count, columns, layers = shape
    return pl.pallas_call(
        functools.partial(analysis_kernel, members, NSITER),
        out_shape=jax.ShapeDtypeStruct(shape, jnp.bfloat16),
        in_specs=[VMEM] * (1 + len(fields)),
        out_specs=VMEM,
        scratch_shapes=[pltpu.VMEM((count * columns, layers), jnp.float32)],
        compiler_params=SMALL,
        name="analysis",
    )(parts, *fields)


def swapped(block, code):
    return lax.ppermute(block, "mem", [(i, i ^ code) for i in range(lax.axis_size("mem"))])


def on_device(
    background_fields, wind_courant, spreading_number, obs_col, obs_lev, obs_value, obs_var
):
    columns = background_fields.shape[1]
    mems, cols, rows = (lax.axis_size(a) for a in ("mem", "col", "row"))
    low, high = neighbours(background_fields, ("row", "col"))
    fields, hx, edges = inner_forecast(
        background_fields, wind_courant, spreading_number, obs_col, obs_lev
    )
    fields, copies = edge_forecast(
        columns, edges, low, high, hx, obs_col, obs_lev, fields, mems
    )
    readings = lax.all_to_all(copies, "mem", 0, 0)
    me = lax.axis_index("mem").astype(jnp.int32).reshape(1)
    near = [swapped(fields, code) for code in (2, 6)]
    parts = gram_parts(me, readings, obs_value, obs_var, rows)
    fields_later, _ = lax.optimization_barrier((fields, parts))
    far = swapped(fields_later, 4)
    other = swapped(fields_later, 1)
    parts = lax.all_to_all(parts, "row", 0, 0)
    parts = sum_copies(parts, cols)
    near[0], near[1], _ = lax.optimization_barrier((*near, parts))
    other_near = [swapped(block, 1) for block in near]
    other_far = swapped(far, 1)
    parts = lax.all_to_all(parts, "col", 0, 0)
    held = (fields, *near, far, other, *other_near, other_far)
    return analysis(parts, held, background_fields.shape)


def solution(mesh):
    grid, mem = mesh.shape["grid"], mesh.shape["mem"]
    fine = Mesh(mesh.devices.reshape(ROWS, grid // ROWS, mem), ("row", "col", "mem"))
    blocks = ("row", "col")
    in_specs = (
        P("mem", blocks, None),
        P(blocks, None),
        P(blocks, None),
        P(blocks),
        P(blocks),
        P(blocks),
        P(blocks),
    )
    out_specs = P("mem", blocks, None)
    return jax.shard_map(
        on_device, mesh=fine, in_specs=in_specs, out_specs=out_specs, check_vma=False
    )
```

```python
import functools

import jax
import jax.numpy as jnp
from jax import lax
from jax.experimental import pallas as pl
from jax.experimental.pallas import tpu as pltpu
from jax.sharding import Mesh, PartitionSpec as P

NSITER = 8
ROWS = 8
LANES = 128
GROUP = 8
ORDER = (0, 2, 6, 4, 1, 3, 7, 5)
EXACT = lax.Precision.HIGHEST
VMEM = pl.BlockSpec(memory_space=pltpu.VMEM)
SMALL = pltpu.CompilerParams(vmem_limit_bytes=16 * 2**20)


def lane_index(rows):
    return lax.broadcasted_iota(jnp.int32, (rows, LANES), 1)


def neighbours(block, axis):
    count = lax.axis_size(axis)
    forward = [(i, i + 1) for i in range(count - 1)]
    backward = [(target, source) for source, target in forward]
    last = block.shape[1] - 1
    low = lax.ppermute(block[:, last:, :], axis, forward)
    high = lax.ppermute(block[:, :1, :], axis, backward)
    return low[:, 0], high[:, 0]


def chosen_levels(lev, layers):
    level = lax.broadcasted_iota(jnp.int32, (layers, lev.shape[0]), 0)
    return jnp.where(level == lev[...].reshape(1, -1), 1.0, 0.0).astype(jnp.bfloat16)


def at_levels(values, chosen):
    rest, picked = values, None
    for _ in range(3):
        part = rest.astype(jnp.bfloat16)
        rest = rest - part.astype(jnp.float32)
        term = jnp.dot(part, chosen, preferred_element_type=jnp.float32)
        picked = term if picked is None else picked + term
    return picked


def inner_kernel(
    columns, field_hbm, courant_hbm, spreading_hbm, col, lev, fields, readings, edges,
    field, courant, spreading, cells, sems,
):
    sources = ((field_hbm, field), (courant_hbm, courant), (spreading_hbm, spreading))
    fetches = [pltpu.make_async_copy(s, d, sems.at[i]) for i, (s, d) in enumerate(sources)]
    for fetch in fetches:
        fetch.start()
    members = fields.shape[0]
    layers = field.shape[1]
    observations = col.shape[0]
    lane = lax.broadcasted_iota(jnp.int32, (members, layers), 1)
    chosen = chosen_levels(lev, layers)
    where_col = jnp.broadcast_to(col[...].reshape(1, -1), (members, observations))
    for fetch in fetches:
        fetch.wait()

    def column(i):
        if i < 0 or i >= columns:
            return jnp.zeros((members, layers), jnp.float32)
        return field[pl.ds(i, members, stride=columns), :]

    left, centre = column(-1), column(0)
    for i in range(columns):
        right = column(i + 1)
        below = jnp.where(lane == 0, 0.0, pltpu.roll(centre, 1, 1))
        above = jnp.where(lane == layers - 1, 0.0, pltpu.roll(centre, layers - 1, 1))
        value = (
            centre
            + courant[pl.ds(i, 1), :] * (left - right) * 0.5
            + spreading[pl.ds(i, 1), :] * (right + left + above + below - 4.0 * centre)
        )
        cells[i * members : (i + 1) * members, :] = value
        fields[:, i * layers : (i + 1) * layers] = value.astype(jnp.bfloat16)
        left, centre = centre, right

    last = columns - 1
    spread = lambda row: jnp.broadcast_to(row, (members, layers))
    edges[0] = cells[:members, :]
    edges[1] = cells[last * members :, :]
    edges[2] = spread(spreading[:1, :] + courant[:1, :] * 0.5)
    edges[3] = spread(spreading[last:, :] - courant[last:, :] * 0.5)

    step = 16
    total = jnp.zeros((members, observations), jnp.float32)
    for base in range(0, columns, step):
        picked = at_levels(cells[base * members : (base + step) * members, :], chosen)
        for i in range(step):
            if 0 < base + i < last:
                row = picked[i * members : (i + 1) * members, :]
                total = total + jnp.where(where_col == base + i, row, 0.0)
    readings[...] = total


def inner_forecast(field, courant, spreading, col, lev):
    members, columns, layers = field.shape
    observations = col.shape[0]
    anywhere = pl.BlockSpec(memory_space=pltpu.HBM)
    return pl.pallas_call(
        functools.partial(inner_kernel, columns),
        out_shape=(
            jax.ShapeDtypeStruct((members, columns * layers), jnp.bfloat16),
            jax.ShapeDtypeStruct((members, observations), jnp.float32),
            jax.ShapeDtypeStruct((4, members, layers), jnp.float32),
        ),
        in_specs=[anywhere] * 3 + [VMEM] * 2,
        out_specs=(VMEM, VMEM, VMEM),
        scratch_shapes=[
            pltpu.VMEM((members * columns, layers), jnp.float32),
            pltpu.VMEM((columns, layers), jnp.float32),
            pltpu.VMEM((columns, layers), jnp.float32),
            pltpu.VMEM((members * columns, layers), jnp.float32),
            pltpu.SemaphoreType.DMA((3,)),
        ],
        compiler_params=SMALL,
        cost_estimate=pl.CostEstimate(
            flops=6 * members * columns * layers * observations,
            bytes_accessed=4 * members * columns * layers,
            transcendentals=0,
        ),
        name="inner_forecast",
    )(field.reshape(members * columns, layers), courant, spreading, col, lev)


def edge_kernel(columns, edges, low, high, readings, col, lev, fields_in, fields, copies):
    del fields_in
    members, layers = low.shape
    observations = col.shape[0]
    first = edges[0] + edges[2] * low[...]
    last = edges[1] + edges[3] * high[...]
    fields[:, :layers] = first.astype(jnp.bfloat16)
    fields[:, (columns - 1) * layers :] = last.astype(jnp.bfloat16)
    picked = at_levels(jnp.concatenate([first, last], axis=0), chosen_levels(lev, layers))
    where_col = jnp.broadcast_to(col[...].reshape(1, -1), (members, observations))
    total = jnp.where(where_col == 0, picked[:members, :], readings[...])
    total = jnp.where(where_col == columns - 1, picked[members:, :], total)
    for r in range(copies.shape[0]):
        copies[r] = total


def edge_forecast(columns, edges, low, high, readings, col, lev, fields, count):
    return pl.pallas_call(
        functools.partial(edge_kernel, columns),
        out_shape=(
            jax.ShapeDtypeStruct(fields.shape, fields.dtype),
            jax.ShapeDtypeStruct((count,) + readings.shape, jnp.float32),
        ),
        in_specs=[VMEM] * 7,
        out_specs=(VMEM, VMEM),
        input_output_aliases={6: 0},
        compiler_params=SMALL,
        name="edge_forecast",
    )(edges, low, high, readings, col, lev, fields)


def pack(upper, proj_row):
    lane = lane_index(GROUP)
    row = [upper[GROUP * r : GROUP * (r + 1), :] for r in range(8)]
    roll = lambda r, shift: pltpu.roll(row[r], shift, 1)
    first = jnp.where(lane < 64, row[0], roll(1, 64))
    second = jnp.where(lane < 16, roll(7, 80), row[2])
    second = jnp.where(lane >= 64, roll(3, 48), second)
    second = jnp.where(lane >= 112, roll(6, 64), second)
    third = jnp.where(lane < 32, roll(5, 96), row[4])
    third = jnp.where(lane >= 64, pltpu.roll(proj_row, 64, 1), third)
    return first, second, third


def unpack(first, second, third):
    lane = lane_index(GROUP)
    roll = lambda part, shift: pltpu.roll(part, shift, 1)
    rows = [
        first,
        roll(first, 64),
        second,
        roll(second, 80),
        third,
        roll(third, 32),
        roll(second, 64),
        roll(second, 48),
    ]
    keep = [
        jnp.where((lane >= 16 * (r // 2)) & (lane < 64), part, 0.0) for r, part in enumerate(rows)
    ]
    upper = jnp.concatenate(keep, axis=0)
    return upper, roll(third, 64)[:1, :]


def gram_kernel(me, readings, value, var, copies):
    hx = jnp.concatenate([readings[me[0] ^ code] for code in ORDER], axis=0)
    members = hx.shape[0]
    ybar = jnp.sum(hx, axis=0, keepdims=True) * (1.0 / members)
    anomaly = hx - ybar
    innov = value[...].reshape(1, -1) - ybar
    weighted = anomaly / var[...].reshape(1, -1)
    pad = jnp.zeros((LANES - members, hx.shape[1]), jnp.float32)
    weighted = jnp.concatenate([weighted, pad], axis=0)
    nt = (((1,), (1,)), ((), ()))
    gram = lax.dot_general(
        anomaly, weighted, nt, precision=EXACT, preferred_element_type=jnp.float32
    )
    rows = jnp.where(
        lax.broadcasted_iota(jnp.int32, (GROUP, hx.shape[1]), 0) == 0,
        jnp.broadcast_to(innov, (GROUP, hx.shape[1])),
        0.0,
    )
    proj = lax.dot_general(
        rows, weighted, nt, precision=EXACT, preferred_element_type=jnp.float32
    )
    for s, part in enumerate(pack(gram, proj)):
        for r in range(copies.shape[0]):
            copies[r, GROUP * s : GROUP * (s + 1), :] = part


def gram_parts(me, readings, value, var, count):
    return pl.pallas_call(
        gram_kernel,
        out_shape=jax.ShapeDtypeStruct((count, 3 * GROUP, LANES), jnp.float32),
        in_specs=[pl.BlockSpec(memory_space=pltpu.SMEM)] + [VMEM] * 3,
        out_specs=VMEM,
        compiler_params=SMALL,
        name="gram",
    )(me, readings, value, var)


def sum_kernel(parts, copies):
    total = parts[0]
    for r in range(1, parts.shape[0]):
        total = total + parts[r]
    for r in range(copies.shape[0]):
        copies[r] = total


def sum_copies(parts, count):
    return pl.pallas_call(
        sum_kernel,
        out_shape=jax.ShapeDtypeStruct((count,) + parts.shape[1:], jnp.float32),
        in_specs=[VMEM],
        out_specs=VMEM,
        compiler_params=SMALL,
        name="row_sum",
    )(parts)


def analysis_kernel(members, iters, parts, *refs):
    *fields, out, cells = refs
    total = parts[0]
    for r in range(1, parts.shape[0]):
        total = total + parts[r]
    upper, proj = unpack(*[total[GROUP * s : GROUP * (s + 1), :] for s in range(3)])
    square = jnp.concatenate(
        [upper, jnp.zeros((LANES - members, LANES), jnp.float32)], axis=0
    )
    turned = square.T
    row = lax.broadcasted_iota(jnp.int32, (LANES, LANES), 0)
    lane = lane_index(LANES)
    gram = jnp.where(lane // 16 >= row // 16, square, turned)[:members, :members]
    row, lane = row[:members, :members], lane[:members, :members]
    eye = jnp.where(row == lane, 1.0, 0.0)
    proj = proj[:, :members]

    dot = lambda a, b: jnp.dot(a, b, precision=EXACT, preferred_element_type=jnp.float32)
    amat = (members - 1.0) * eye + gram
    scale = jnp.sqrt(jnp.sum(amat * amat, keepdims=True))
    yit = amat / scale
    zit = eye
    for step in range(iters):
        if step == 0:
            tmat = (3.0 * eye - yit) * 0.5
        else:
            tmat = (3.0 * eye - dot(zit, yit)) * 0.5
        if step + 1 < iters:
            yit = dot(yit, tmat)
        zit = tmat if step == 0 else dot(tmat, zit)
    root = zit / jnp.sqrt(scale)
    turned = root.T
    wmean = dot(dot(proj, turned), turned)
    tfm = wmean + jnp.sqrt(jnp.float32(members - 1.0)) * turned
    centre = jnp.sum(tfm, axis=1, keepdims=True) * (1.0 / members)
    mixed = 1.0 / members + tfm - centre

    count, columns, layers = out.shape
    mine = mixed[:count, :].astype(jnp.bfloat16)
    step = 16
    for base in range(0, columns, step):
        held = [part[:, base * layers : (base + step) * layers] for part in fields]
        block = jnp.dot(
            mine, jnp.concatenate(held, axis=0), preferred_element_type=jnp.float32
        )
        for i in range(step):
            cells[pl.ds(base + i, count, stride=columns), :] = block[
                :, i * layers : (i + 1) * layers
            ]
    out[...] = cells[...].astype(jnp.bfloat16).reshape(out.shape)


def analysis(parts, fields, shape):
    members = sum(part.shape[0] for part in fields)
    count, columns, layers = shape
    return pl.pallas_call(
        functools.partial(analysis_kernel, members, NSITER),
        out_shape=jax.ShapeDtypeStruct(shape, jnp.bfloat16),
        in_specs=[VMEM] * (1 + len(fields)),
        out_specs=VMEM,
        scratch_shapes=[pltpu.VMEM((count * columns, layers), jnp.float32)],
        compiler_params=SMALL,
        name="analysis",
    )(parts, *fields)


def swapped(block, code):
    return lax.ppermute(block, "mem", [(i, i ^ code) for i in range(lax.axis_size("mem"))])


def on_device(
    background_fields, wind_courant, spreading_number, obs_col, obs_lev, obs_value, obs_var
):
    columns = background_fields.shape[1]
    mems, cols, rows = (lax.axis_size(a) for a in ("mem", "col", "row"))
    low, high = neighbours(background_fields, ("row", "col"))
    fields, hx, edges = inner_forecast(
        background_fields, wind_courant, spreading_number, obs_col, obs_lev
    )
    fields, copies = edge_forecast(
        columns, edges, low, high, hx, obs_col, obs_lev, fields, mems
    )
    readings = lax.all_to_all(copies, "mem", 0, 0)
    me = lax.axis_index("mem").astype(jnp.int32).reshape(1)
    beside = swapped(fields, 2)
    parts = gram_parts(me, readings, obs_value, obs_var, rows)
    fields_later, _ = lax.optimization_barrier((fields, parts))
    beside, _ = lax.optimization_barrier((beside, parts))
    pair = jnp.concatenate([fields, beside], axis=0)
    pair_other = swapped(pair, 1)
    far = [swapped(block, 6) for block in (fields_later, beside)]
    parts = lax.all_to_all(parts, "row", 0, 0)
    parts = sum_copies(parts, cols)
    far[0], far[1], _ = lax.optimization_barrier((*far, parts))
    others = [swapped(block, 1) for block in far]
    parts = lax.all_to_all(parts, "col", 0, 0)
    held = (pair, *far, pair_other, *others)
    return analysis(parts, held, background_fields.shape)


def solution(mesh):
    grid, mem = mesh.shape["grid"], mesh.shape["mem"]
    fine = Mesh(mesh.devices.reshape(ROWS, grid // ROWS, mem), ("row", "col", "mem"))
    blocks = ("row", "col")
    in_specs = (
        P("mem", blocks, None),
        P(blocks, None),
        P(blocks, None),
        P(blocks),
        P(blocks),
        P(blocks),
        P(blocks),
    )
    out_specs = P("mem", blocks, None)
    return jax.shard_map(
        on_device, mesh=fine, in_specs=in_specs, out_specs=out_specs, check_vma=False
    )
```

```python
import functools

import jax
import jax.numpy as jnp
from jax import lax
from jax.experimental import pallas as pl
from jax.experimental.pallas import tpu as pltpu
from jax.sharding import Mesh, PartitionSpec as P

NSITER = 8
ROWS = 8
LANES = 128
GROUP = 8
ORDER = (0, 2, 6, 4, 1, 3, 7, 5)
EXACT = lax.Precision.HIGHEST
VMEM = pl.BlockSpec(memory_space=pltpu.VMEM)
SMALL = pltpu.CompilerParams(vmem_limit_bytes=16 * 2**20)


def lane_index(rows):
    return lax.broadcasted_iota(jnp.int32, (rows, LANES), 1)


def neighbours(block, axis):
    count = lax.axis_size(axis)
    forward = [(i, i + 1) for i in range(count - 1)]
    backward = [(target, source) for source, target in forward]
    last = block.shape[1] - 1
    low = lax.ppermute(block[:, last:, :], axis, forward)
    high = lax.ppermute(block[:, :1, :], axis, backward)
    return low[:, 0], high[:, 0]


def chosen_levels(lev, layers):
    level = lax.broadcasted_iota(jnp.int32, (layers, lev.shape[0]), 0)
    return jnp.where(level == lev[...].reshape(1, -1), 1.0, 0.0).astype(jnp.bfloat16)


def at_levels(values, chosen):
    rest, picked = values, None
    for _ in range(3):
        part = rest.astype(jnp.bfloat16)
        rest = rest - part.astype(jnp.float32)
        term = jnp.dot(part, chosen, preferred_element_type=jnp.float32)
        picked = term if picked is None else picked + term
    return picked


def inner_kernel(
    columns, field_hbm, courant_hbm, spreading_hbm, col, lev, fields, readings, edges,
    field, courant, spreading, cells, sems,
):
    sources = ((field_hbm, field), (courant_hbm, courant), (spreading_hbm, spreading))
    fetches = [pltpu.make_async_copy(s, d, sems.at[i]) for i, (s, d) in enumerate(sources)]
    for fetch in fetches:
        fetch.start()
    members = fields.shape[0]
    layers = field.shape[1]
    observations = col.shape[0]
    lane = lax.broadcasted_iota(jnp.int32, (members, layers), 1)
    chosen = chosen_levels(lev, layers)
    where_col = jnp.broadcast_to(col[...].reshape(1, -1), (members, observations))
    for fetch in fetches:
        fetch.wait()

    def column(i):
        if i < 0 or i >= columns:
            return jnp.zeros((members, layers), jnp.float32)
        return field[pl.ds(i, members, stride=columns), :]

    left, centre = column(-1), column(0)
    for i in range(columns):
        right = column(i + 1)
        below = jnp.where(lane == 0, 0.0, pltpu.roll(centre, 1, 1))
        above = jnp.where(lane == layers - 1, 0.0, pltpu.roll(centre, layers - 1, 1))
        value = (
            centre
            + courant[pl.ds(i, 1), :] * (left - right) * 0.5
            + spreading[pl.ds(i, 1), :] * (right + left + above + below - 4.0 * centre)
        )
        cells[i * members : (i + 1) * members, :] = value
        fields[:, i * layers : (i + 1) * layers] = value.astype(jnp.bfloat16)
        left, centre = centre, right

    last = columns - 1
    spread = lambda row: jnp.broadcast_to(row, (members, layers))
    edges[0] = cells[:members, :]
    edges[1] = cells[last * members :, :]
    edges[2] = spread(spreading[:1, :] + courant[:1, :] * 0.5)
    edges[3] = spread(spreading[last:, :] - courant[last:, :] * 0.5)

    step = 16
    total = jnp.zeros((members, observations), jnp.float32)
    for base in range(0, columns, step):
        picked = at_levels(cells[base * members : (base + step) * members, :], chosen)
        for i in range(step):
            if 0 < base + i < last:
                row = picked[i * members : (i + 1) * members, :]
                total = total + jnp.where(where_col == base + i, row, 0.0)
    readings[...] = total


def inner_forecast(field, courant, spreading, col, lev):
    members, columns, layers = field.shape
    observations = col.shape[0]
    anywhere = pl.BlockSpec(memory_space=pltpu.HBM)
    return pl.pallas_call(
        functools.partial(inner_kernel, columns),
        out_shape=(
            jax.ShapeDtypeStruct((members, columns * layers), jnp.bfloat16),
            jax.ShapeDtypeStruct((members, observations), jnp.float32),
            jax.ShapeDtypeStruct((4, members, layers), jnp.float32),
        ),
        in_specs=[anywhere] * 3 + [VMEM] * 2,
        out_specs=(VMEM, VMEM, VMEM),
        scratch_shapes=[
            pltpu.VMEM((members * columns, layers), jnp.float32),
            pltpu.VMEM((columns, layers), jnp.float32),
            pltpu.VMEM((columns, layers), jnp.float32),
            pltpu.VMEM((members * columns, layers), jnp.float32),
            pltpu.SemaphoreType.DMA((3,)),
        ],
        compiler_params=SMALL,
        cost_estimate=pl.CostEstimate(
            flops=6 * members * columns * layers * observations,
            bytes_accessed=4 * members * columns * layers,
            transcendentals=0,
        ),
        name="inner_forecast",
    )(field.reshape(members * columns, layers), courant, spreading, col, lev)


def edge_kernel(columns, edges, low, high, readings, col, lev, fields_in, fields, copies):
    del fields_in
    members, layers = low.shape
    observations = col.shape[0]
    first = edges[0] + edges[2] * low[...]
    last = edges[1] + edges[3] * high[...]
    fields[:, :layers] = first.astype(jnp.bfloat16)
    fields[:, (columns - 1) * layers :] = last.astype(jnp.bfloat16)
    picked = at_levels(jnp.concatenate([first, last], axis=0), chosen_levels(lev, layers))
    where_col = jnp.broadcast_to(col[...].reshape(1, -1), (members, observations))
    total = jnp.where(where_col == 0, picked[:members, :], readings[...])
    total = jnp.where(where_col == columns - 1, picked[members:, :], total)
    for r in range(copies.shape[0]):
        copies[r] = total


def edge_forecast(columns, edges, low, high, readings, col, lev, fields, count):
    return pl.pallas_call(
        functools.partial(edge_kernel, columns),
        out_shape=(
            jax.ShapeDtypeStruct(fields.shape, fields.dtype),
            jax.ShapeDtypeStruct((count,) + readings.shape, jnp.float32),
        ),
        in_specs=[VMEM] * 7,
        out_specs=(VMEM, VMEM),
        input_output_aliases={6: 0},
        compiler_params=SMALL,
        name="edge_forecast",
    )(edges, low, high, readings, col, lev, fields)


def pack(upper, proj_row):
    lane = lane_index(GROUP)
    row = [upper[GROUP * r : GROUP * (r + 1), :] for r in range(8)]
    roll = lambda r, shift: pltpu.roll(row[r], shift, 1)
    first = jnp.where(lane < 64, row[0], roll(1, 64))
    second = jnp.where(lane < 16, roll(7, 80), row[2])
    second = jnp.where(lane >= 64, roll(3, 48), second)
    second = jnp.where(lane >= 112, roll(6, 64), second)
    third = jnp.where(lane < 32, roll(5, 96), row[4])
    third = jnp.where(lane >= 64, pltpu.roll(proj_row, 64, 1), third)
    return first, second, third


def unpack(first, second, third):
    lane = lane_index(GROUP)
    roll = lambda part, shift: pltpu.roll(part, shift, 1)
    rows = [
        first,
        roll(first, 64),
        second,
        roll(second, 80),
        third,
        roll(third, 32),
        roll(second, 64),
        roll(second, 48),
    ]
    keep = [
        jnp.where((lane >= 16 * (r // 2)) & (lane < 64), part, 0.0) for r, part in enumerate(rows)
    ]
    upper = jnp.concatenate(keep, axis=0)
    return upper, roll(third, 64)[:1, :]


def gram_kernel(me, readings, value, var, copies):
    hx = jnp.concatenate([readings[me[0] ^ code] for code in ORDER], axis=0)
    members = hx.shape[0]
    ybar = jnp.sum(hx, axis=0, keepdims=True) * (1.0 / members)
    anomaly = hx - ybar
    innov = value[...].reshape(1, -1) - ybar
    weighted = anomaly / var[...].reshape(1, -1)
    pad = jnp.zeros((LANES - members, hx.shape[1]), jnp.float32)
    weighted = jnp.concatenate([weighted, pad], axis=0)
    nt = (((1,), (1,)), ((), ()))
    gram = lax.dot_general(
        anomaly, weighted, nt, precision=EXACT, preferred_element_type=jnp.float32
    )
    rows = jnp.where(
        lax.broadcasted_iota(jnp.int32, (GROUP, hx.shape[1]), 0) == 0,
        jnp.broadcast_to(innov, (GROUP, hx.shape[1])),
        0.0,
    )
    proj = lax.dot_general(
        rows, weighted, nt, precision=EXACT, preferred_element_type=jnp.float32
    )
    for s, part in enumerate(pack(gram, proj)):
        for r in range(copies.shape[0]):
            copies[r, GROUP * s : GROUP * (s + 1), :] = part


def gram_parts(me, readings, value, var, count):
    return pl.pallas_call(
        gram_kernel,
        out_shape=jax.ShapeDtypeStruct((count, 3 * GROUP, LANES), jnp.float32),
        in_specs=[pl.BlockSpec(memory_space=pltpu.SMEM)] + [VMEM] * 3,
        out_specs=VMEM,
        compiler_params=SMALL,
        name="gram",
    )(me, readings, value, var)


def sum_kernel(parts, copies):
    total = parts[0]
    for r in range(1, parts.shape[0]):
        total = total + parts[r]
    rows = total.shape[0]
    spare = jnp.zeros((copies.shape[1] - rows, total.shape[1]), jnp.float32)
    for r in range(copies.shape[0]):
        copies[r, :rows] = total
        copies[r, rows:] = spare


def sum_copies(parts, count):
    return pl.pallas_call(
        sum_kernel,
        out_shape=jax.ShapeDtypeStruct((count, 40, LANES), jnp.float32),
        in_specs=[VMEM],
        out_specs=VMEM,
        compiler_params=SMALL,
        name="row_sum",
    )(parts)


def analysis_kernel(members, iters, parts, *refs):
    *fields, out, cells = refs
    total = parts[0]
    for r in range(1, parts.shape[0]):
        total = total + parts[r]
    upper, proj = unpack(*[total[GROUP * s : GROUP * (s + 1), :] for s in range(3)])
    square = jnp.concatenate(
        [upper, jnp.zeros((LANES - members, LANES), jnp.float32)], axis=0
    )
    turned = square.T
    row = lax.broadcasted_iota(jnp.int32, (LANES, LANES), 0)
    lane = lane_index(LANES)
    gram = jnp.where(lane // 16 >= row // 16, square, turned)[:members, :members]
    row, lane = row[:members, :members], lane[:members, :members]
    eye = jnp.where(row == lane, 1.0, 0.0)
    proj = proj[:, :members]

    dot = lambda a, b: jnp.dot(a, b, precision=EXACT, preferred_element_type=jnp.float32)
    amat = (members - 1.0) * eye + gram
    scale = jnp.sqrt(jnp.sum(amat * amat, keepdims=True))
    yit = amat / scale
    zit = eye
    for step in range(iters):
        if step == 0:
            tmat = (3.0 * eye - yit) * 0.5
        else:
            tmat = (3.0 * eye - dot(zit, yit)) * 0.5
        if step + 1 < iters:
            yit = dot(yit, tmat)
        zit = tmat if step == 0 else dot(tmat, zit)
    root = zit / jnp.sqrt(scale)
    turned = root.T
    wmean = dot(dot(proj, turned), turned)
    tfm = wmean + jnp.sqrt(jnp.float32(members - 1.0)) * turned
    centre = jnp.sum(tfm, axis=1, keepdims=True) * (1.0 / members)
    mixed = 1.0 / members + tfm - centre

    count, columns, layers = out.shape
    mine = mixed[:count, :].astype(jnp.bfloat16)
    step = 16
    for base in range(0, columns, step):
        held = [part[:, base * layers : (base + step) * layers] for part in fields]
        block = jnp.dot(
            mine, jnp.concatenate(held, axis=0), preferred_element_type=jnp.float32
        )
        for i in range(step):
            cells[pl.ds(base + i, count, stride=columns), :] = block[
                :, i * layers : (i + 1) * layers
            ]
    out[...] = cells[...].astype(jnp.bfloat16).reshape(out.shape)


def analysis(parts, fields, shape):
    members = sum(part.shape[0] for part in fields)
    count, columns, layers = shape
    return pl.pallas_call(
        functools.partial(analysis_kernel, members, NSITER),
        out_shape=jax.ShapeDtypeStruct(shape, jnp.bfloat16),
        in_specs=[VMEM] * (1 + len(fields)),
        out_specs=VMEM,
        scratch_shapes=[pltpu.VMEM((count * columns, layers), jnp.float32)],
        compiler_params=SMALL,
        name="analysis",
    )(parts, *fields)


def swapped(block, code):
    return lax.ppermute(block, "mem", [(i, i ^ code) for i in range(lax.axis_size("mem"))])


def on_device(
    background_fields, wind_courant, spreading_number, obs_col, obs_lev, obs_value, obs_var
):
    columns = background_fields.shape[1]
    mems, cols, rows = (lax.axis_size(a) for a in ("mem", "col", "row"))
    low, high = neighbours(background_fields, ("row", "col"))
    fields, hx, edges = inner_forecast(
        background_fields, wind_courant, spreading_number, obs_col, obs_lev
    )
    fields, copies = edge_forecast(
        columns, edges, low, high, hx, obs_col, obs_lev, fields, mems
    )
    readings = lax.all_to_all(copies, "mem", 0, 0)
    me = lax.axis_index("mem").astype(jnp.int32).reshape(1)
    beside = swapped(fields, 2)
    parts = gram_parts(me, readings, obs_value, obs_var, cols)
    fields_later, _ = lax.optimization_barrier((fields, parts))
    beside, _ = lax.optimization_barrier((beside, parts))
    pair = jnp.concatenate([fields, beside], axis=0)
    pair_other = swapped(pair, 1)
    far = [swapped(block, 6) for block in (fields_later, beside)]
    parts = lax.all_to_all(parts, "col", 0, 0)
    parts = sum_copies(parts, rows)
    far[0], far[1], _ = lax.optimization_barrier((*far, parts))
    others = [swapped(block, 1) for block in far]
    parts = lax.all_to_all(parts, "row", 0, 0)
    held = (pair, *far, pair_other, *others)
    return analysis(parts, held, background_fields.shape)


def solution(mesh):
    grid, mem = mesh.shape["grid"], mesh.shape["mem"]
    fine = Mesh(mesh.devices.reshape(ROWS, grid // ROWS, mem), ("row", "col", "mem"))
    blocks = ("row", "col")
    in_specs = (
        P("mem", blocks, None),
        P(blocks, None),
        P(blocks, None),
        P(blocks),
        P(blocks),
        P(blocks),
        P(blocks),
    )
    out_specs = P("mem", blocks, None)
    return jax.shard_map(
        on_device, mesh=fine, in_specs=in_specs, out_specs=out_specs, check_vma=False
    )
```

```python
import functools

import jax
import jax.numpy as jnp
from jax import lax
from jax.experimental import pallas as pl
from jax.experimental.pallas import tpu as pltpu
from jax.sharding import Mesh, PartitionSpec as P

NSITER = 8
ROWS = 8
LANES = 128
GROUP = 8
ORDER = (0, 2, 6, 4, 1, 3, 7, 5)
EXACT = lax.Precision.HIGHEST
VMEM = pl.BlockSpec(memory_space=pltpu.VMEM)
SMALL = pltpu.CompilerParams(vmem_limit_bytes=16 * 2**20)


def lane_index(rows):
    return lax.broadcasted_iota(jnp.int32, (rows, LANES), 1)


def neighbours(block, axis):
    count = lax.axis_size(axis)
    forward = [(i, i + 1) for i in range(count - 1)]
    backward = [(target, source) for source, target in forward]
    last = block.shape[1] - 1
    low = lax.ppermute(block[:, last:, :], axis, forward)
    high = lax.ppermute(block[:, :1, :], axis, backward)
    return low[:, 0], high[:, 0]


def chosen_levels(lev, layers):
    level = lax.broadcasted_iota(jnp.int32, (layers, lev.shape[0]), 0)
    return jnp.where(level == lev[...].reshape(1, -1), 1.0, 0.0).astype(jnp.bfloat16)


def at_levels(values, chosen):
    rest, picked = values, None
    for _ in range(3):
        part = rest.astype(jnp.bfloat16)
        rest = rest - part.astype(jnp.float32)
        term = jnp.dot(part, chosen, preferred_element_type=jnp.float32)
        picked = term if picked is None else picked + term
    return picked


def inner_kernel(
    columns, field, leftward, rightward, col, lev, fields, readings, edges, cells
):
    members = fields.shape[0]
    layers = field.shape[1]
    observations = col.shape[0]
    lane = lax.broadcasted_iota(jnp.int32, (members, layers), 1)
    chosen = chosen_levels(lev, layers)
    where_col = jnp.broadcast_to(col[...].reshape(1, -1), (members, observations))

    def column(i):
        if i < 0 or i >= columns:
            return jnp.zeros((members, layers), jnp.float32)
        return field[pl.ds(i, members, stride=columns), :]

    left, centre = column(-1), column(0)
    for i in range(columns):
        right = column(i + 1)
        below = jnp.where(lane == 0, 0.0, pltpu.roll(centre, 1, 1))
        above = jnp.where(lane == layers - 1, 0.0, pltpu.roll(centre, layers - 1, 1))
        from_left, from_right = leftward[pl.ds(i, 1), :], rightward[pl.ds(i, 1), :]
        value = (
            centre
            + from_left * left
            + from_right * right
            + 0.5 * (from_left + from_right) * (above + below - 4.0 * centre)
        )
        cells[i * members : (i + 1) * members, :] = value
        fields[:, i * layers : (i + 1) * layers] = value.astype(jnp.bfloat16)
        left, centre = centre, right

    last = columns - 1
    spread = lambda row: jnp.broadcast_to(row, (members, layers))
    edges[0] = cells[:members, :]
    edges[1] = cells[last * members :, :]
    edges[2] = spread(leftward[:1, :])
    edges[3] = spread(rightward[last:, :])

    step = 16
    total = jnp.zeros((members, observations), jnp.float32)
    for base in range(0, columns, step):
        picked = at_levels(cells[base * members : (base + step) * members, :], chosen)
        for i in range(step):
            if 0 < base + i < last:
                row = picked[i * members : (i + 1) * members, :]
                total = total + jnp.where(where_col == base + i, row, 0.0)
    readings[...] = total


def inner_forecast(field, leftward, rightward, col, lev):
    members, columns, layers = field.shape
    observations = col.shape[0]
    return pl.pallas_call(
        functools.partial(inner_kernel, columns),
        out_shape=(
            jax.ShapeDtypeStruct((members, columns * layers), jnp.bfloat16),
            jax.ShapeDtypeStruct((members, observations), jnp.float32),
            jax.ShapeDtypeStruct((4, members, layers), jnp.float32),
        ),
        in_specs=[VMEM] * 5,
        out_specs=(VMEM, VMEM, VMEM),
        scratch_shapes=[
            pltpu.VMEM((members * columns, layers), jnp.float32),
        ],
        compiler_params=SMALL,
        cost_estimate=pl.CostEstimate(
            flops=6 * members * columns * layers * observations,
            bytes_accessed=4 * members * columns * layers,
            transcendentals=0,
        ),
        name="inner_forecast",
    )(field.reshape(members * columns, layers), leftward, rightward, col, lev)


def edge_kernel(columns, edges, low, high, readings, col, lev, fields_in, fields, copies):
    del fields_in
    members, layers = low.shape
    observations = col.shape[0]
    first = edges[0] + edges[2] * low[...]
    last = edges[1] + edges[3] * high[...]
    fields[:, :layers] = first.astype(jnp.bfloat16)
    fields[:, (columns - 1) * layers :] = last.astype(jnp.bfloat16)
    picked = at_levels(jnp.concatenate([first, last], axis=0), chosen_levels(lev, layers))
    where_col = jnp.broadcast_to(col[...].reshape(1, -1), (members, observations))
    total = jnp.where(where_col == 0, picked[:members, :], readings[...])
    total = jnp.where(where_col == columns - 1, picked[members:, :], total)
    for r in range(copies.shape[0]):
        copies[r] = total


def edge_forecast(columns, edges, low, high, readings, col, lev, fields, count):
    return pl.pallas_call(
        functools.partial(edge_kernel, columns),
        out_shape=(
            jax.ShapeDtypeStruct(fields.shape, fields.dtype),
            jax.ShapeDtypeStruct((count,) + readings.shape, jnp.float32),
        ),
        in_specs=[VMEM] * 7,
        out_specs=(VMEM, VMEM),
        input_output_aliases={6: 0},
        compiler_params=SMALL,
        name="edge_forecast",
    )(edges, low, high, readings, col, lev, fields)


def pack(upper, proj_row):
    lane = lane_index(GROUP)
    row = [upper[GROUP * r : GROUP * (r + 1), :] for r in range(8)]
    roll = lambda r, shift: pltpu.roll(row[r], shift, 1)
    first = jnp.where(lane < 64, row[0], roll(1, 64))
    second = jnp.where(lane < 16, roll(7, 80), row[2])
    second = jnp.where(lane >= 64, roll(3, 48), second)
    second = jnp.where(lane >= 112, roll(6, 64), second)
    third = jnp.where(lane < 32, roll(5, 96), row[4])
    third = jnp.where(lane >= 64, pltpu.roll(proj_row, 64, 1), third)
    return first, second, third


def unpack(first, second, third):
    lane = lane_index(GROUP)
    roll = lambda part, shift: pltpu.roll(part, shift, 1)
    rows = [
        first,
        roll(first, 64),
        second,
        roll(second, 80),
        third,
        roll(third, 32),
        roll(second, 64),
        roll(second, 48),
    ]
    keep = [
        jnp.where((lane >= 16 * (r // 2)) & (lane < 64), part, 0.0) for r, part in enumerate(rows)
    ]
    upper = jnp.concatenate(keep, axis=0)
    return upper, roll(third, 64)[:1, :]


def gram_kernel(me, readings, value, var, copies):
    hx = jnp.concatenate([readings[me[0] ^ code] for code in ORDER], axis=0)
    members = hx.shape[0]
    ybar = jnp.sum(hx, axis=0, keepdims=True) * (1.0 / members)
    anomaly = hx - ybar
    innov = value[...].reshape(1, -1) - ybar
    weighted = anomaly / var[...].reshape(1, -1)
    pad = jnp.zeros((LANES - members, hx.shape[1]), jnp.float32)
    weighted = jnp.concatenate([weighted, pad], axis=0)
    nt = (((1,), (1,)), ((), ()))
    gram = lax.dot_general(
        anomaly, weighted, nt, precision=EXACT, preferred_element_type=jnp.float32
    )
    rows = jnp.where(
        lax.broadcasted_iota(jnp.int32, (GROUP, hx.shape[1]), 0) == 0,
        jnp.broadcast_to(innov, (GROUP, hx.shape[1])),
        0.0,
    )
    proj = lax.dot_general(
        rows, weighted, nt, precision=EXACT, preferred_element_type=jnp.float32
    )
    for s, part in enumerate(pack(gram, proj)):
        for r in range(copies.shape[0]):
            copies[r, GROUP * s : GROUP * (s + 1), :] = part


def gram_parts(me, readings, value, var, count):
    return pl.pallas_call(
        gram_kernel,
        out_shape=jax.ShapeDtypeStruct((count, 3 * GROUP, LANES), jnp.float32),
        in_specs=[pl.BlockSpec(memory_space=pltpu.SMEM)] + [VMEM] * 3,
        out_specs=VMEM,
        compiler_params=SMALL,
        name="gram",
    )(me, readings, value, var)


def sum_kernel(parts, copies):
    total = parts[0]
    for r in range(1, parts.shape[0]):
        total = total + parts[r]
    rows = total.shape[0]
    spare = jnp.zeros((copies.shape[1] - rows, total.shape[1]), jnp.float32)
    for r in range(copies.shape[0]):
        copies[r, :rows] = total
        copies[r, rows:] = spare


def sum_copies(parts, count):
    return pl.pallas_call(
        sum_kernel,
        out_shape=jax.ShapeDtypeStruct((count, 40, LANES), jnp.float32),
        in_specs=[VMEM],
        out_specs=VMEM,
        compiler_params=SMALL,
        name="row_sum",
    )(parts)


def mix_kernel(members, iters, count, parts, mix):
    total = parts[0]
    for r in range(1, parts.shape[0]):
        total = total + parts[r]
    upper, proj = unpack(*[total[GROUP * s : GROUP * (s + 1), :] for s in range(3)])
    square = jnp.concatenate(
        [upper, jnp.zeros((LANES - members, LANES), jnp.float32)], axis=0
    )
    turned = square.T
    row = lax.broadcasted_iota(jnp.int32, (LANES, LANES), 0)
    lane = lane_index(LANES)
    gram = jnp.where(lane // 16 >= row // 16, square, turned)[:members, :members]
    row, lane = row[:members, :members], lane[:members, :members]
    eye = jnp.where(row == lane, 1.0, 0.0)
    proj = proj[:, :members]

    dot = lambda a, b: jnp.dot(a, b, precision=EXACT, preferred_element_type=jnp.float32)
    amat = (members - 1.0) * eye + gram
    scale = jnp.sqrt(jnp.sum(amat * amat, keepdims=True))
    yit = amat / scale
    zit = eye
    for step in range(iters):
        if step == 0:
            tmat = (3.0 * eye - yit) * 0.5
        else:
            tmat = (3.0 * eye - dot(zit, yit)) * 0.5
        if step + 1 < iters:
            yit = dot(yit, tmat)
        zit = tmat if step == 0 else dot(tmat, zit)
    root = zit / jnp.sqrt(scale)
    turned = root.T
    wmean = dot(dot(proj, turned), turned)
    tfm = wmean + jnp.sqrt(jnp.float32(members - 1.0)) * turned
    centre = jnp.sum(tfm, axis=1, keepdims=True) * (1.0 / members)
    mixed = 1.0 / members + tfm - centre

    mix[...] = mixed[:count, :].astype(jnp.bfloat16)


def analysis_kernel(mix, *refs):
    *fields, out, cells = refs
    count, columns, layers = out.shape
    mine = mix[...]
    step = 16
    for base in range(0, columns, step):
        held = [part[:, base * layers : (base + step) * layers] for part in fields]
        block = jnp.dot(
            mine, jnp.concatenate(held, axis=0), preferred_element_type=jnp.float32
        )
        for i in range(step):
            cells[pl.ds(base + i, count, stride=columns), :] = block[
                :, i * layers : (i + 1) * layers
            ]
    out[...] = cells[...].astype(jnp.bfloat16).reshape(out.shape)


def analysis(parts, fields, shape):
    members = sum(part.shape[0] for part in fields)
    count, columns, layers = shape
    mix = pl.pallas_call(
        functools.partial(mix_kernel, members, NSITER, count),
        out_shape=jax.ShapeDtypeStruct((count, members), jnp.bfloat16),
        in_specs=[VMEM],
        out_specs=VMEM,
        compiler_params=SMALL,
        name="mix",
    )(parts)
    return pl.pallas_call(
        analysis_kernel,
        out_shape=jax.ShapeDtypeStruct(shape, jnp.bfloat16),
        in_specs=[VMEM] * (1 + len(fields)),
        out_specs=VMEM,
        scratch_shapes=[pltpu.VMEM((count * columns, layers), jnp.float32)],
        compiler_params=SMALL,
        name="analysis",
    )(mix, *fields)


def swapped(block, code):
    return lax.ppermute(block, "mem", [(i, i ^ code) for i in range(lax.axis_size("mem"))])


def on_device(
    background_fields, wind_courant, spreading_number, obs_col, obs_lev, obs_value, obs_var
):
    columns = background_fields.shape[1]
    mems, cols, rows = (lax.axis_size(a) for a in ("mem", "col", "row"))
    low, high = neighbours(background_fields, ("row", "col"))
    fields, hx, edges = inner_forecast(
        background_fields,
        spreading_number + wind_courant * 0.5,
        spreading_number - wind_courant * 0.5,
        obs_col,
        obs_lev,
    )
    fields, copies = edge_forecast(
        columns, edges, low, high, hx, obs_col, obs_lev, fields, mems
    )
    readings = lax.all_to_all(copies, "mem", 0, 0)
    me = lax.axis_index("mem").astype(jnp.int32).reshape(1)
    beside = swapped(fields, 2)
    parts = gram_parts(me, readings, obs_value, obs_var, cols)
    fields_later, _ = lax.optimization_barrier((fields, parts))
    beside, _ = lax.optimization_barrier((beside, parts))
    pair = jnp.concatenate([fields, beside], axis=0)
    pair_other = swapped(pair, 1)
    far = [swapped(block, 6) for block in (fields_later, beside)]
    parts = lax.all_to_all(parts, "col", 0, 0)
    parts = sum_copies(parts, rows)
    far[0], far[1], _ = lax.optimization_barrier((*far, parts))
    others = [swapped(block, 1) for block in far]
    parts = lax.all_to_all(parts, "row", 0, 0)
    held = (pair, *far, pair_other, *others)
    return analysis(parts, held, background_fields.shape)


def solution(mesh):
    grid, mem = mesh.shape["grid"], mesh.shape["mem"]
    fine = Mesh(mesh.devices.reshape(ROWS, grid // ROWS, mem), ("row", "col", "mem"))
    blocks = ("row", "col")
    in_specs = (
        P("mem", blocks, None),
        P(blocks, None),
        P(blocks, None),
        P(blocks),
        P(blocks),
        P(blocks),
        P(blocks),
    )
    out_specs = P("mem", blocks, None)
    return jax.shard_map(
        on_device, mesh=fine, in_specs=in_specs, out_specs=out_specs, check_vma=False
    )
```

```python
import functools

import jax
import jax.numpy as jnp
from jax import lax
from jax.experimental import pallas as pl
from jax.experimental.pallas import tpu as pltpu
from jax.sharding import Mesh, PartitionSpec as P

NSITER = 8
PIECES = 4
ROWS = 8
LANES = 128
GROUP = 8
ORDER = (0, 2, 6, 4, 1, 3, 7, 5)
EXACT = lax.Precision.HIGHEST
VMEM = pl.BlockSpec(memory_space=pltpu.VMEM)
SMALL = pltpu.CompilerParams(vmem_limit_bytes=16 * 2**20)


def lane_index(rows):
    return lax.broadcasted_iota(jnp.int32, (rows, LANES), 1)


def neighbours(block, axis):
    count = lax.axis_size(axis)
    forward = [(i, i + 1) for i in range(count - 1)]
    backward = [(target, source) for source, target in forward]
    last = block.shape[1] - 1
    low = lax.ppermute(block[:, last:, :], axis, forward)
    high = lax.ppermute(block[:, :1, :], axis, backward)
    return low[:, 0], high[:, 0]


def chosen_levels(lev, layers):
    level = lax.broadcasted_iota(jnp.int32, (layers, lev.shape[0]), 0)
    return jnp.where(level == lev[...].reshape(1, -1), 1.0, 0.0).astype(jnp.bfloat16)


def at_levels(values, chosen):
    rest, picked = values, None
    for _ in range(3):
        part = rest.astype(jnp.bfloat16)
        rest = rest - part.astype(jnp.float32)
        term = jnp.dot(part, chosen, preferred_element_type=jnp.float32)
        picked = term if picked is None else picked + term
    return picked


def inner_kernel(
    columns, field, leftward, rightward, col, lev, fields, readings, edges, cells
):
    members = fields.shape[0]
    layers = field.shape[1]
    observations = col.shape[0]
    lane = lax.broadcasted_iota(jnp.int32, (members, layers), 1)
    chosen = chosen_levels(lev, layers)
    where_col = jnp.broadcast_to(col[...].reshape(1, -1), (members, observations))

    def column(i):
        if i < 0 or i >= columns:
            return jnp.zeros((members, layers), jnp.float32)
        return field[pl.ds(i, members, stride=columns), :]

    left, centre = column(-1), column(0)
    for i in range(columns):
        right = column(i + 1)
        below = jnp.where(lane == 0, 0.0, pltpu.roll(centre, 1, 1))
        above = jnp.where(lane == layers - 1, 0.0, pltpu.roll(centre, layers - 1, 1))
        from_left, from_right = leftward[pl.ds(i, 1), :], rightward[pl.ds(i, 1), :]
        value = (
            centre
            + from_left * left
            + from_right * right
            + 0.5 * (from_left + from_right) * (above + below - 4.0 * centre)
        )
        cells[i * members : (i + 1) * members, :] = value
        fields[:, i * layers : (i + 1) * layers] = value.astype(jnp.bfloat16)
        left, centre = centre, right

    last = columns - 1
    spread = lambda row: jnp.broadcast_to(row, (members, layers))
    edges[0] = cells[:members, :]
    edges[1] = cells[last * members :, :]
    edges[2] = spread(leftward[:1, :])
    edges[3] = spread(rightward[last:, :])

    step = 16
    total = jnp.zeros((members, observations), jnp.float32)
    for base in range(0, columns, step):
        picked = at_levels(cells[base * members : (base + step) * members, :], chosen)
        for i in range(step):
            if 0 < base + i < last:
                row = picked[i * members : (i + 1) * members, :]
                total = total + jnp.where(where_col == base + i, row, 0.0)
    readings[...] = total


def inner_forecast(field, leftward, rightward, col, lev):
    members, columns, layers = field.shape
    observations = col.shape[0]
    return pl.pallas_call(
        functools.partial(inner_kernel, columns),
        out_shape=(
            jax.ShapeDtypeStruct((members, columns * layers), jnp.bfloat16),
            jax.ShapeDtypeStruct((members, observations), jnp.float32),
            jax.ShapeDtypeStruct((4, members, layers), jnp.float32),
        ),
        in_specs=[VMEM] * 5,
        out_specs=(VMEM, VMEM, VMEM),
        scratch_shapes=[
            pltpu.VMEM((members * columns, layers), jnp.float32),
        ],
        compiler_params=SMALL,
        cost_estimate=pl.CostEstimate(
            flops=6 * members * columns * layers * observations,
            bytes_accessed=4 * members * columns * layers,
            transcendentals=0,
        ),
        name="inner_forecast",
    )(field.reshape(members * columns, layers), leftward, rightward, col, lev)


def edge_kernel(columns, edges, low, high, readings, col, lev, fields_in, fields, copies):
    del fields_in
    members, layers = low.shape
    observations = col.shape[0]
    first = edges[0] + edges[2] * low[...]
    last = edges[1] + edges[3] * high[...]
    fields[:, :layers] = first.astype(jnp.bfloat16)
    fields[:, (columns - 1) * layers :] = last.astype(jnp.bfloat16)
    picked = at_levels(jnp.concatenate([first, last], axis=0), chosen_levels(lev, layers))
    where_col = jnp.broadcast_to(col[...].reshape(1, -1), (members, observations))
    total = jnp.where(where_col == 0, picked[:members, :], readings[...])
    total = jnp.where(where_col == columns - 1, picked[members:, :], total)
    for r in range(copies.shape[0]):
        copies[r] = total


def edge_forecast(columns, edges, low, high, readings, col, lev, fields, count):
    return pl.pallas_call(
        functools.partial(edge_kernel, columns),
        out_shape=(
            jax.ShapeDtypeStruct(fields.shape, fields.dtype),
            jax.ShapeDtypeStruct((count,) + readings.shape, jnp.float32),
        ),
        in_specs=[VMEM] * 7,
        out_specs=(VMEM, VMEM),
        input_output_aliases={6: 0},
        compiler_params=SMALL,
        name="edge_forecast",
    )(edges, low, high, readings, col, lev, fields)


def pack(upper, proj_row):
    lane = lane_index(GROUP)
    row = [upper[GROUP * r : GROUP * (r + 1), :] for r in range(8)]
    roll = lambda r, shift: pltpu.roll(row[r], shift, 1)
    first = jnp.where(lane < 64, row[0], roll(1, 64))
    second = jnp.where(lane < 16, roll(7, 80), row[2])
    second = jnp.where(lane >= 64, roll(3, 48), second)
    second = jnp.where(lane >= 112, roll(6, 64), second)
    third = jnp.where(lane < 32, roll(5, 96), row[4])
    third = jnp.where(lane >= 64, pltpu.roll(proj_row, 64, 1), third)
    return first, second, third


def unpack(first, second, third):
    lane = lane_index(GROUP)
    roll = lambda part, shift: pltpu.roll(part, shift, 1)
    rows = [
        first,
        roll(first, 64),
        second,
        roll(second, 80),
        third,
        roll(third, 32),
        roll(second, 64),
        roll(second, 48),
    ]
    keep = [
        jnp.where((lane >= 16 * (r // 2)) & (lane < 64), part, 0.0) for r, part in enumerate(rows)
    ]
    upper = jnp.concatenate(keep, axis=0)
    return upper, roll(third, 64)[:1, :]


def gram_kernel(me, readings, value, var, copies):
    hx = jnp.concatenate([readings[me[0] ^ code] for code in ORDER], axis=0)
    members = hx.shape[0]
    ybar = jnp.sum(hx, axis=0, keepdims=True) * (1.0 / members)
    anomaly = hx - ybar
    innov = value[...].reshape(1, -1) - ybar
    weighted = anomaly / var[...].reshape(1, -1)
    pad = jnp.zeros((LANES - members, hx.shape[1]), jnp.float32)
    weighted = jnp.concatenate([weighted, pad], axis=0)
    nt = (((1,), (1,)), ((), ()))
    gram = lax.dot_general(
        anomaly, weighted, nt, precision=EXACT, preferred_element_type=jnp.float32
    )
    rows = jnp.where(
        lax.broadcasted_iota(jnp.int32, (GROUP, hx.shape[1]), 0) == 0,
        jnp.broadcast_to(innov, (GROUP, hx.shape[1])),
        0.0,
    )
    proj = lax.dot_general(
        rows, weighted, nt, precision=EXACT, preferred_element_type=jnp.float32
    )
    for s, part in enumerate(pack(gram, proj)):
        for r in range(copies.shape[0]):
            copies[r, GROUP * s : GROUP * (s + 1), :] = part


def gram_parts(me, readings, value, var, count):
    return pl.pallas_call(
        gram_kernel,
        out_shape=jax.ShapeDtypeStruct((count, 3 * GROUP, LANES), jnp.float32),
        in_specs=[pl.BlockSpec(memory_space=pltpu.SMEM)] + [VMEM] * 3,
        out_specs=VMEM,
        compiler_params=SMALL,
        name="gram",
    )(me, readings, value, var)


def sum_kernel(parts, copies):
    total = parts[0]
    for r in range(1, parts.shape[0]):
        total = total + parts[r]
    rows = total.shape[0]
    spare = jnp.zeros((copies.shape[1] - rows, total.shape[1]), jnp.float32)
    for r in range(copies.shape[0]):
        copies[r, :rows] = total
        copies[r, rows:] = spare


def sum_copies(parts, count):
    return pl.pallas_call(
        sum_kernel,
        out_shape=jax.ShapeDtypeStruct((count, 40, LANES), jnp.float32),
        in_specs=[VMEM],
        out_specs=VMEM,
        compiler_params=SMALL,
        name="row_sum",
    )(parts)


def mix_kernel(members, iters, count, parts, mix):
    total = parts[0]
    for r in range(1, parts.shape[0]):
        total = total + parts[r]
    upper, proj = unpack(*[total[GROUP * s : GROUP * (s + 1), :] for s in range(3)])
    square = jnp.concatenate(
        [upper, jnp.zeros((LANES - members, LANES), jnp.float32)], axis=0
    )
    turned = square.T
    row = lax.broadcasted_iota(jnp.int32, (LANES, LANES), 0)
    lane = lane_index(LANES)
    gram = jnp.where(lane // 16 >= row // 16, square, turned)[:members, :members]
    row, lane = row[:members, :members], lane[:members, :members]
    eye = jnp.where(row == lane, 1.0, 0.0)
    proj = proj[:, :members]

    dot = lambda a, b: jnp.dot(a, b, precision=EXACT, preferred_element_type=jnp.float32)
    amat = (members - 1.0) * eye + gram
    scale = jnp.sqrt(jnp.sum(amat * amat, keepdims=True))
    yit = amat / scale
    zit = eye
    for step in range(iters):
        if step == 0:
            tmat = (3.0 * eye - yit) * 0.5
        else:
            tmat = (3.0 * eye - dot(zit, yit)) * 0.5
        if step + 1 < iters:
            yit = dot(yit, tmat)
        zit = tmat if step == 0 else dot(tmat, zit)
    root = zit / jnp.sqrt(scale)
    turned = root.T
    wmean = dot(dot(proj, turned), turned)
    tfm = wmean + jnp.sqrt(jnp.float32(members - 1.0)) * turned
    centre = jnp.sum(tfm, axis=1, keepdims=True) * (1.0 / members)
    mixed = 1.0 / members + tfm - centre

    mix[...] = mixed[:count, :].astype(jnp.bfloat16)


def analysis_kernel(mix, *refs):
    *fields, out, cells, stage, sems = refs
    count, columns, layers = out.shape
    mine = mix[...]
    step = 16
    width = columns // PIECES
    writes = []
    for piece in range(PIECES):
        first = piece * width
        for base in range(first, first + width, step):
            held = [part[:, base * layers : (base + step) * layers] for part in fields]
            block = jnp.dot(
                mine, jnp.concatenate(held, axis=0), preferred_element_type=jnp.float32
            )
            for i in range(step):
                cells[pl.ds(base + i, count, stride=columns), :] = block[
                    :, i * layers : (i + 1) * layers
                ]
        for m in range(count):
            low = m * columns + first
            stage[m, first : first + width, :] = cells[low : low + width, :].astype(jnp.bfloat16)
        window = pl.ds(first, width)
        writes.append(
            pltpu.make_async_copy(stage.at[:, window, :], out.at[:, window, :], sems.at[piece])
        )
        writes[-1].start()
    for write in writes:
        write.wait()


def analysis(parts, fields, shape):
    members = sum(part.shape[0] for part in fields)
    count, columns, layers = shape
    mix = pl.pallas_call(
        functools.partial(mix_kernel, members, NSITER, count),
        out_shape=jax.ShapeDtypeStruct((count, members), jnp.bfloat16),
        in_specs=[VMEM],
        out_specs=VMEM,
        compiler_params=SMALL,
        name="mix",
    )(parts)
    return pl.pallas_call(
        analysis_kernel,
        out_shape=jax.ShapeDtypeStruct(shape, jnp.bfloat16),
        in_specs=[VMEM] * (1 + len(fields)),
        out_specs=pl.BlockSpec(memory_space=pl.ANY),
        scratch_shapes=[
            pltpu.VMEM((count * columns, layers), jnp.float32),
            pltpu.VMEM(shape, jnp.bfloat16),
            pltpu.SemaphoreType.DMA((PIECES,)),
        ],
        compiler_params=SMALL,
        name="analysis",
    )(mix, *fields)


def swapped(block, code):
    return lax.ppermute(block, "mem", [(i, i ^ code) for i in range(lax.axis_size("mem"))])


def on_device(
    background_fields, wind_courant, spreading_number, obs_col, obs_lev, obs_value, obs_var
):
    columns = background_fields.shape[1]
    mems, cols, rows = (lax.axis_size(a) for a in ("mem", "col", "row"))
    low, high = neighbours(background_fields, ("row", "col"))
    fields, hx, edges = inner_forecast(
        background_fields,
        spreading_number + wind_courant * 0.5,
        spreading_number - wind_courant * 0.5,
        obs_col,
        obs_lev,
    )
    fields, copies = edge_forecast(
        columns, edges, low, high, hx, obs_col, obs_lev, fields, mems
    )
    readings = lax.all_to_all(copies, "mem", 0, 0)
    me = lax.axis_index("mem").astype(jnp.int32).reshape(1)
    beside = swapped(fields, 2)
    parts = gram_parts(me, readings, obs_value, obs_var, cols)
    fields_later, _ = lax.optimization_barrier((fields, parts))
    beside, _ = lax.optimization_barrier((beside, parts))
    pair = jnp.concatenate([fields, beside], axis=0)
    pair_other = swapped(pair, 1)
    far = [swapped(block, 6) for block in (fields_later, beside)]
    parts = lax.all_to_all(parts, "col", 0, 0)
    parts = sum_copies(parts, rows)
    far[0], far[1], _ = lax.optimization_barrier((*far, parts))
    others = [swapped(block, 1) for block in far]
    parts = lax.all_to_all(parts, "row", 0, 0)
    held = (pair, *far, pair_other, *others)
    return analysis(parts, held, background_fields.shape)


def solution(mesh):
    grid, mem = mesh.shape["grid"], mesh.shape["mem"]
    fine = Mesh(mesh.devices.reshape(ROWS, grid // ROWS, mem), ("row", "col", "mem"))
    blocks = ("row", "col")
    in_specs = (
        P("mem", blocks, None),
        P(blocks, None),
        P(blocks, None),
        P(blocks),
        P(blocks),
        P(blocks),
        P(blocks),
    )
    out_specs = P("mem", blocks, None)
    return jax.shard_map(
        on_device, mesh=fine, in_specs=in_specs, out_specs=out_specs, check_vma=False
    )
```

```python
import functools

import jax
import jax.numpy as jnp
from jax import lax
from jax.experimental import pallas as pl
from jax.experimental.pallas import tpu as pltpu
from jax.sharding import Mesh, PartitionSpec as P

NSITER = 8
ROWS = 8
LANES = 128
GROUP = 8
ORDER = (0, 2, 6, 4, 1, 3, 7, 5)
EXACT = lax.Precision.HIGHEST
VMEM = pl.BlockSpec(memory_space=pltpu.VMEM)
SMALL = pltpu.CompilerParams(vmem_limit_bytes=16 * 2**20)


def lane_index(rows):
    return lax.broadcasted_iota(jnp.int32, (rows, LANES), 1)


def neighbours(block, axis):
    count = lax.axis_size(axis)
    forward = [(i, i + 1) for i in range(count - 1)]
    backward = [(target, source) for source, target in forward]
    last = block.shape[1] - 1
    high = lax.ppermute(block[:, :1, :], axis, backward)
    low = lax.ppermute(block[:, last:, :], axis, forward)
    return low[:, 0], high[:, 0]


def chosen_levels(lev, layers):
    level = lax.broadcasted_iota(jnp.int32, (layers, lev.shape[0]), 0)
    return jnp.where(level == lev[...].reshape(1, -1), 1.0, 0.0).astype(jnp.bfloat16)


def at_levels(values, chosen):
    rest, picked = values, None
    for _ in range(3):
        part = rest.astype(jnp.bfloat16)
        rest = rest - part.astype(jnp.float32)
        term = jnp.dot(part, chosen, preferred_element_type=jnp.float32)
        picked = term if picked is None else picked + term
    return picked


def inner_kernel(
    columns, field, leftward, rightward, col, lev, fields, readings, edges, cells
):
    members = fields.shape[0]
    layers = field.shape[1]
    observations = col.shape[0]
    lane = lax.broadcasted_iota(jnp.int32, (members, layers), 1)
    chosen = chosen_levels(lev, layers)
    where_col = jnp.broadcast_to(col[...].reshape(1, -1), (members, observations))

    def column(i):
        if i < 0 or i >= columns:
            return jnp.zeros((members, layers), jnp.float32)
        return field[pl.ds(i, members, stride=columns), :]

    left, centre = column(-1), column(0)
    for i in range(columns):
        right = column(i + 1)
        below = jnp.where(lane == 0, 0.0, pltpu.roll(centre, 1, 1))
        above = jnp.where(lane == layers - 1, 0.0, pltpu.roll(centre, layers - 1, 1))
        from_left, from_right = leftward[pl.ds(i, 1), :], rightward[pl.ds(i, 1), :]
        value = (
            centre
            + from_left * left
            + from_right * right
            + 0.5 * (from_left + from_right) * (above + below - 4.0 * centre)
        )
        cells[i * members : (i + 1) * members, :] = value
        fields[:, i * layers : (i + 1) * layers] = value.astype(jnp.bfloat16)
        left, centre = centre, right

    last = columns - 1
    spread = lambda row: jnp.broadcast_to(row, (members, layers))
    edges[0] = cells[:members, :]
    edges[1] = cells[last * members :, :]
    edges[2] = spread(leftward[:1, :])
    edges[3] = spread(rightward[last:, :])

    step = 16
    total = jnp.zeros((members, observations), jnp.float32)
    for base in range(0, columns, step):
        picked = at_levels(cells[base * members : (base + step) * members, :], chosen)
        for i in range(step):
            if 0 < base + i < last:
                row = picked[i * members : (i + 1) * members, :]
                total = total + jnp.where(where_col == base + i, row, 0.0)
    readings[...] = total


def inner_forecast(field, leftward, rightward, col, lev):
    members, columns, layers = field.shape
    observations = col.shape[0]
    return pl.pallas_call(
        functools.partial(inner_kernel, columns),
        out_shape=(
            jax.ShapeDtypeStruct((members, columns * layers), jnp.bfloat16),
            jax.ShapeDtypeStruct((members, observations), jnp.float32),
            jax.ShapeDtypeStruct((4, members, layers), jnp.float32),
        ),
        in_specs=[VMEM] * 5,
        out_specs=(VMEM, VMEM, VMEM),
        scratch_shapes=[
            pltpu.VMEM((members * columns, layers), jnp.float32),
        ],
        compiler_params=SMALL,
        cost_estimate=pl.CostEstimate(
            flops=6 * members * columns * layers * observations,
            bytes_accessed=4 * members * columns * layers,
            transcendentals=0,
        ),
        name="inner_forecast",
    )(field.reshape(members * columns, layers), leftward, rightward, col, lev)


def edge_kernel(columns, edges, low, high, readings, col, lev, fields_in, fields, copies):
    del fields_in
    members, layers = low.shape
    observations = col.shape[0]
    first = edges[0] + edges[2] * low[...]
    last = edges[1] + edges[3] * high[...]
    fields[:, :layers] = first.astype(jnp.bfloat16)
    fields[:, (columns - 1) * layers :] = last.astype(jnp.bfloat16)
    picked = at_levels(jnp.concatenate([first, last], axis=0), chosen_levels(lev, layers))
    where_col = jnp.broadcast_to(col[...].reshape(1, -1), (members, observations))
    total = jnp.where(where_col == 0, picked[:members, :], readings[...])
    total = jnp.where(where_col == columns - 1, picked[members:, :], total)
    for r in range(copies.shape[0]):
        copies[r] = total


def edge_forecast(columns, edges, low, high, readings, col, lev, fields, count):
    return pl.pallas_call(
        functools.partial(edge_kernel, columns),
        out_shape=(
            jax.ShapeDtypeStruct(fields.shape, fields.dtype),
            jax.ShapeDtypeStruct((count,) + readings.shape, jnp.float32),
        ),
        in_specs=[VMEM] * 7,
        out_specs=(VMEM, VMEM),
        input_output_aliases={6: 0},
        compiler_params=SMALL,
        name="edge_forecast",
    )(edges, low, high, readings, col, lev, fields)


def pack(upper, proj_row):
    lane = lane_index(GROUP)
    row = [upper[GROUP * r : GROUP * (r + 1), :] for r in range(8)]
    roll = lambda r, shift: pltpu.roll(row[r], shift, 1)
    first = jnp.where(lane < 64, row[0], roll(1, 64))
    second = jnp.where(lane < 16, roll(7, 80), row[2])
    second = jnp.where(lane >= 64, roll(3, 48), second)
    second = jnp.where(lane >= 112, roll(6, 64), second)
    third = jnp.where(lane < 32, roll(5, 96), row[4])
    third = jnp.where(lane >= 64, pltpu.roll(proj_row, 64, 1), third)
    return first, second, third


def unpack(first, second, third):
    lane = lane_index(GROUP)
    roll = lambda part, shift: pltpu.roll(part, shift, 1)
    rows = [
        first,
        roll(first, 64),
        second,
        roll(second, 80),
        third,
        roll(third, 32),
        roll(second, 64),
        roll(second, 48),
    ]
    keep = [
        jnp.where((lane >= 16 * (r // 2)) & (lane < 64), part, 0.0) for r, part in enumerate(rows)
    ]
    upper = jnp.concatenate(keep, axis=0)
    return upper, roll(third, 64)[:1, :]


def gram_kernel(me, readings, value, var, copies):
    hx = jnp.concatenate([readings[me[0] ^ code] for code in ORDER], axis=0)
    members = hx.shape[0]
    ybar = jnp.sum(hx, axis=0, keepdims=True) * (1.0 / members)
    anomaly = hx - ybar
    innov = value[...].reshape(1, -1) - ybar
    weighted = anomaly / var[...].reshape(1, -1)
    pad = jnp.zeros((LANES - members, hx.shape[1]), jnp.float32)
    weighted = jnp.concatenate([weighted, pad], axis=0)
    nt = (((1,), (1,)), ((), ()))
    gram = lax.dot_general(
        anomaly, weighted, nt, precision=EXACT, preferred_element_type=jnp.float32
    )
    rows = jnp.where(
        lax.broadcasted_iota(jnp.int32, (GROUP, hx.shape[1]), 0) == 0,
        jnp.broadcast_to(innov, (GROUP, hx.shape[1])),
        0.0,
    )
    proj = lax.dot_general(
        rows, weighted, nt, precision=EXACT, preferred_element_type=jnp.float32
    )
    for s, part in enumerate(pack(gram, proj)):
        for r in range(copies.shape[0]):
            copies[r, GROUP * s : GROUP * (s + 1), :] = part


def gram_parts(me, readings, value, var, count):
    return pl.pallas_call(
        gram_kernel,
        out_shape=jax.ShapeDtypeStruct((count, 3 * GROUP, LANES), jnp.float32),
        in_specs=[pl.BlockSpec(memory_space=pltpu.SMEM)] + [VMEM] * 3,
        out_specs=VMEM,
        compiler_params=SMALL,
        name="gram",
    )(me, readings, value, var)


def sum_kernel(parts, copies):
    total = parts[0]
    for r in range(1, parts.shape[0]):
        total = total + parts[r]
    rows = total.shape[0]
    spare = jnp.zeros((copies.shape[1] - rows, total.shape[1]), jnp.float32)
    for r in range(copies.shape[0]):
        copies[r, :rows] = total
        copies[r, rows:] = spare


def sum_copies(parts, count):
    return pl.pallas_call(
        sum_kernel,
        out_shape=jax.ShapeDtypeStruct((count, 40, LANES), jnp.float32),
        in_specs=[VMEM],
        out_specs=VMEM,
        compiler_params=SMALL,
        name="row_sum",
    )(parts)


def mix_kernel(members, iters, count, parts, mix):
    total = parts[0]
    for r in range(1, parts.shape[0]):
        total = total + parts[r]
    upper, proj = unpack(*[total[GROUP * s : GROUP * (s + 1), :] for s in range(3)])
    square = jnp.concatenate(
        [upper, jnp.zeros((LANES - members, LANES), jnp.float32)], axis=0
    )
    turned = square.T
    row = lax.broadcasted_iota(jnp.int32, (LANES, LANES), 0)
    lane = lane_index(LANES)
    gram = jnp.where(lane // 16 >= row // 16, square, turned)[:members, :members]
    row, lane = row[:members, :members], lane[:members, :members]
    eye = jnp.where(row == lane, 1.0, 0.0)
    proj = proj[:, :members]

    dot = lambda a, b: jnp.dot(a, b, precision=EXACT, preferred_element_type=jnp.float32)
    amat = (members - 1.0) * eye + gram
    scale = jnp.sqrt(jnp.sum(amat * amat, keepdims=True))
    yit = amat / scale
    zit = eye
    for step in range(iters):
        if step == 0:
            tmat = (3.0 * eye - yit) * 0.5
        else:
            tmat = (3.0 * eye - dot(zit, yit)) * 0.5
        if step + 1 < iters:
            yit = dot(yit, tmat)
        zit = tmat if step == 0 else dot(tmat, zit)
    root = zit / jnp.sqrt(scale)
    turned = root.T
    wmean = dot(dot(proj, turned), turned)
    tfm = wmean + jnp.sqrt(jnp.float32(members - 1.0)) * turned
    centre = jnp.sum(tfm, axis=1, keepdims=True) * (1.0 / members)
    mixed = 1.0 / members + tfm - centre

    mix[...] = mixed[:count, :].astype(jnp.bfloat16)


def analysis_kernel(mix, *refs):
    *fields, out, cells = refs
    count, columns, layers = out.shape
    mine = mix[...]
    step = 16
    for base in range(0, columns, step):
        held = [part[:, base * layers : (base + step) * layers] for part in fields]
        block = jnp.dot(
            mine, jnp.concatenate(held, axis=0), preferred_element_type=jnp.float32
        )
        for i in range(step):
            cells[pl.ds(base + i, count, stride=columns), :] = block[
                :, i * layers : (i + 1) * layers
            ]
    out[...] = cells[...].astype(jnp.bfloat16).reshape(out.shape)


def analysis(parts, fields, shape):
    members = sum(part.shape[0] for part in fields)
    count, columns, layers = shape
    mix = pl.pallas_call(
        functools.partial(mix_kernel, members, NSITER, count),
        out_shape=jax.ShapeDtypeStruct((count, members), jnp.bfloat16),
        in_specs=[VMEM],
        out_specs=VMEM,
        compiler_params=SMALL,
        name="mix",
    )(parts)
    return pl.pallas_call(
        analysis_kernel,
        out_shape=jax.ShapeDtypeStruct(shape, jnp.bfloat16),
        in_specs=[VMEM] * (1 + len(fields)),
        out_specs=VMEM,
        scratch_shapes=[pltpu.VMEM((count * columns, layers), jnp.float32)],
        compiler_params=SMALL,
        name="analysis",
    )(mix, *fields)


def swapped(block, code):
    return lax.ppermute(block, "mem", [(i, i ^ code) for i in range(lax.axis_size("mem"))])


def on_device(
    background_fields, wind_courant, spreading_number, obs_col, obs_lev, obs_value, obs_var
):
    columns = background_fields.shape[1]
    mems, cols, rows = (lax.axis_size(a) for a in ("mem", "col", "row"))
    low, high = neighbours(background_fields, ("row", "col"))
    fields, hx, edges = inner_forecast(
        background_fields,
        spreading_number + wind_courant * 0.5,
        spreading_number - wind_courant * 0.5,
        obs_col,
        obs_lev,
    )
    fields, copies = edge_forecast(
        columns, edges, low, high, hx, obs_col, obs_lev, fields, mems
    )
    readings = lax.all_to_all(copies, "mem", 0, 0)
    me = lax.axis_index("mem").astype(jnp.int32).reshape(1)
    beside = swapped(fields, 2)
    parts = gram_parts(me, readings, obs_value, obs_var, cols)
    fields_later, _ = lax.optimization_barrier((fields, parts))
    beside, _ = lax.optimization_barrier((beside, parts))
    pair = jnp.concatenate([fields, beside], axis=0)
    pair_other = swapped(pair, 1)
    far = [swapped(block, 6) for block in (fields_later, beside)]
    parts = lax.all_to_all(parts, "col", 0, 0)
    parts = sum_copies(parts, rows)
    far[0], far[1], _ = lax.optimization_barrier((*far, parts))
    others = [swapped(block, 1) for block in far]
    parts = lax.all_to_all(parts, "row", 0, 0)
    held = (pair, *far, pair_other, *others)
    return analysis(parts, held, background_fields.shape)


def solution(mesh):
    grid, mem = mesh.shape["grid"], mesh.shape["mem"]
    fine = Mesh(mesh.devices.reshape(ROWS, grid // ROWS, mem), ("row", "col", "mem"))
    blocks = ("row", "col")
    in_specs = (
        P("mem", blocks, None),
        P(blocks, None),
        P(blocks, None),
        P(blocks),
        P(blocks),
        P(blocks),
        P(blocks),
    )
    out_specs = P("mem", blocks, None)
    return jax.shard_map(
        on_device, mesh=fine, in_specs=in_specs, out_specs=out_specs, check_vma=False
    )
```
